128 devices in a mesh: ctx: 32 (over y, x, core), head: 4 (over z).
Axes of the slice: x: 4, y: 4, z: 4, core: 2. Of those that a mesh axis runs over, the one named last changes fastest.
Arguments:
- query_rows: bfloat16 [16384, 8192], P('ctx', 'head'), may hold values from -6 to 6
- key_rows: bfloat16 [16384, 8192], P('ctx', 'head'), may hold values from -6 to 6
- value_rows: bfloat16 [16384, 8192], P('ctx', 'head'), may hold values from -6 to 6
- out_grad: bfloat16 [16384, 8192], P('ctx', 'head'), may hold values from -6 to 6
- norm_gain: float32 [8192], P('head'), may hold values from 0.5 to 1.5
Outputs:
- query_grad: bfloat16 [16384, 8192], P('ctx', 'head')
- key_grad: bfloat16 [16384, 8192], P('ctx', 'head')
- value_grad: bfloat16 [16384, 8192], P('ctx', 'head')
The draws below stay inside these ranges and needn't reach their ends.
All inputs are finite; a program needn't handle non-finite values.
Results may differ from the reference program's by a relative error of at most 0.0059.
Values sent between devices are 32-bit elements; how exact they have to be, the bound alone decides.
No kernel may reach another device: no remote copies, remote signals or barrier semaphores. Data moves between devices by JAX's collectives and lax.ppermute only.
A program may use at most 192 MiB of HBM per device.

```python
import jax
import jax.numpy as jnp
from jax import lax

HEADS = 64
DH = 128
TOK_DEV = 512
D = 8192
TOKENS = 16384


def block_scale(key, shape, pieces, low, high):
    def one(dim, shards_of):
        heights = jax.random.uniform(jax.random.fold_in(jax.random.fold_in(key, 6), dim), (shards_of,), jnp.float32, low / len(pieces), high / len(pieces))
        return jnp.repeat(jnp.exp(heights), shape[dim] // shards_of).reshape((-1,) + (1,) * (len(shape) - dim - 1))

    factor_of = one(*pieces[0])
    for cut in pieces[1:]:
        factor_of = factor_of * one(*cut)
    return factor_of


def noise(stream_key, dims, width, limit, shards=(), kind=jnp.bfloat16):
    values = width * jax.random.normal(stream_key, dims, jnp.float32)
    if shards:
        values = values * block_scale(stream_key, dims, shards, -0.22, 0.18)
    return jnp.clip(values, -limit, limit).astype(kind)


def setup_inputs(seed: int = 0) -> dict:
    arg_keys = jax.random.split(jax.random.key(seed), 6)
    return {
        "query_rows": noise(arg_keys[0], (TOKENS, D), 1.0, 6.0, ((0, 32), (1, 4))),
        "key_rows": noise(arg_keys[1], (TOKENS, D), 1.0, 6.0, ((0, 32), (1, 4))),
        "value_rows": noise(arg_keys[2], (TOKENS, D), 1.0, 6.0, ((0, 32), (1, 4))),
        "out_grad": noise(arg_keys[3], (TOKENS, D), 1.0, 6.0, ((0, 32), (1, 4))),
        "norm_gain": jnp.clip(1.0 + 0.1 * jax.random.normal(arg_keys[4], (D,), jnp.float32), 0.5, 1.5),
    }


epsilon = 1e-06

def split_heads(array):
    blocks = TOKENS // TOK_DEV
    return array.reshape(blocks, TOK_DEV, HEADS, DH).transpose(2, 0, 1, 3)

def join_heads(array):
    return array.transpose(1, 2, 0, 3).reshape(TOKENS, HEADS * DH)

def causal_mask():
    places = lax.broadcasted_iota(jnp.int32, (TOK_DEV, TOK_DEV), 0)
    others = lax.broadcasted_iota(jnp.int32, (TOK_DEV, TOK_DEV), 1)
    return others <= places

def head_scores(query_data, key_data):
    scores = jnp.einsum('cti,csi->cts', query_data.astype(jnp.float32), key_data.astype(jnp.float32))
    return jnp.where(causal_mask()[None], scores, 0.0).astype(jnp.bfloat16)

def head_prefix(key_data, value_data):
    local_state = jnp.einsum('cti,ctj->cij', key_data.astype(jnp.float32), value_data.astype(jnp.float32))
    summed = jnp.cumsum(local_state, axis=0)
    zero_state = jnp.zeros((1, DH, DH), jnp.float32)
    return jnp.concatenate([zero_state, summed[:-1]], axis=0).astype(jnp.bfloat16)

def head_forward(inputs):
    query_data, key_data, value_data = inputs
    prefix_half = head_prefix(key_data, value_data)
    score_half = head_scores(query_data, key_data)
    output = jnp.einsum('cts,csj->ctj', score_half.astype(jnp.float32), value_data.astype(jnp.float32))
    output = output + jnp.einsum('cti,cij->ctj', query_data.astype(jnp.float32), prefix_half.astype(jnp.float32))
    return output

def head_backward(inputs):
    query_data, key_data, value_data, grad_out = inputs
    query_full = query_data.astype(jnp.float32)
    key_full = key_data.astype(jnp.float32)
    value_full = value_data.astype(jnp.float32)
    grad_full = grad_out.astype(jnp.float32)
    prefix_full = head_prefix(key_data, value_data).astype(jnp.float32)
    score_full = head_scores(query_data, key_data).astype(jnp.float32)
    local_grad = jnp.einsum('cti,ctj->cij', query_full, grad_full)
    summed = jnp.cumsum(local_grad[::-1], axis=0)[::-1]
    zero_state = jnp.zeros((1, DH, DH), jnp.float32)
    later_full = jnp.concatenate([summed[1:], zero_state], axis=0).astype(jnp.bfloat16).astype(jnp.float32)
    mixing = jnp.einsum('ctj,csj->cts', grad_full, value_full)
    mixing = jnp.where(causal_mask()[None], mixing, 0.0).astype(jnp.bfloat16).astype(jnp.float32)
    query_grad = jnp.einsum('cts,csi->cti', mixing, key_full) + jnp.einsum('ctj,cij->cti', grad_full, prefix_full)
    key_grad = jnp.einsum('cts,cti->csi', mixing, query_full) + jnp.einsum('csj,cij->csi', value_full, later_full)
    value_grad = jnp.einsum('cts,ctj->csj', score_full, grad_full) + jnp.einsum('csi,cij->csj', key_full, later_full)
    return (query_grad.astype(jnp.bfloat16), key_grad.astype(jnp.bfloat16), value_grad.astype(jnp.bfloat16))

def reference(query_rows, key_rows, value_rows, out_grad, norm_gain):
    query_data = split_heads(query_rows)
    key_data = split_heads(key_rows)
    value_data = split_heads(value_rows)
    output = lax.map(head_forward, (query_data, key_data, value_data))
    gain_data = norm_gain.reshape(HEADS, 1, 1, DH)
    scaled = split_heads(out_grad).astype(jnp.float32) * gain_data
    squares = lax.optimization_barrier(jnp.sum(output * output, axis=(0, 3)))
    products = lax.optimization_barrier(jnp.sum(scaled * output, axis=(0, 3)))
    radius = jnp.sqrt(squares / D + epsilon)
    coeff = products / (D * radius * radius)
    grad_out = ((scaled - output * coeff[None, :, :, None]) / radius[None, :, :, None]).astype(jnp.bfloat16)
    query_grad, key_grad, value_grad = lax.map(head_backward, (query_data, key_data, value_data, grad_out))
    return (join_heads(query_grad), join_heads(key_grad), join_heads(value_grad))
```

```python
import functools

import jax
import jax.numpy as jnp
from jax import lax
from jax.experimental import pallas as pl
from jax.experimental.pallas import tpu as pltpu
from jax.sharding import PartitionSpec as P

DH = 128
BLOCK = 512
HALF = 256
HEADS_LOCAL = 16
WIDTH = HEADS_LOCAL * DH
WIDTH_ALL = 8192
PAIRS = HEADS_LOCAL // 2
SIDE = PAIRS // 2
ROWS = HEADS_LOCAL * DH // 2
CHIPS = 16
SLICE = ROWS // CHIPS
LIMIT = 24 * 1024 * 1024

epsilon = 1e-06

F32 = jnp.float32
BF16 = jnp.bfloat16


def dot(a, b):
    return lax.dot_general(a, b, (((1,), (0,)), ((), ())), preferred_element_type=F32)


def dot_nt(a, b):
    return lax.dot_general(a, b, (((1,), (1,)), ((), ())), preferred_element_type=F32)


def dot_tn(a, b):
    return lax.dot_general(a, b, (((0,), (0,)), ((), ())), preferred_element_type=F32)


def columns(step, core):
    return (0, jnp.bitwise_xor(core[0], step // SIDE) * SIDE + step % SIDE)


def token_spec():
    return pl.BlockSpec((BLOCK, 2 * DH), columns)


def state_spec():
    return pl.BlockSpec((1, 2 * DH, DH), lambda step, core: (step // SIDE, step % SIDE, 0))


def half_spec(which):
    def place(step, core):
        if which == 0:
            return (jnp.minimum(step, SIDE - 1), 0)
        return (jnp.maximum(step - SIDE, 0), 0)

    return pl.BlockSpec((2 * DH, DH), place)


def call(body, in_specs, out_specs, out_shape, flops, bytes_accessed, scratch=()):
    return pl.pallas_call(
        body,
        grid_spec=pltpu.PrefetchScalarGridSpec(
            num_scalar_prefetch=1,
            grid=(PAIRS,),
            in_specs=in_specs,
            out_specs=out_specs,
            scratch_shapes=list(scratch),
        ),
        out_shape=out_shape,
        compiler_params=pltpu.CompilerParams(
            vmem_limit_bytes=LIMIT, dimension_semantics=("arbitrary",)
        ),
        cost_estimate=pl.CostEstimate(
            flops=flops, bytes_accessed=bytes_accessed, transcendentals=0
        ),
    )


def shape(dims, kind):
    return jax.ShapeDtypeStruct(dims, kind)


MIB = 1024 * 1024
STATES = shape((2, ROWS, DH), F32)
TOKENS_F32 = shape((BLOCK, WIDTH), F32)
TOKENS_BF16 = shape((BLOCK, WIDTH), BF16)


def store_states(out, a, b):
    both = dot_tn(a, b)
    out[0, :DH, :] = both[:DH, :DH]
    out[0, DH:, :] = both[DH:, DH:]


def local_state_body(core, k, v, out):
    store_states(out, k[...], v[...])


def lower(array):
    rows = lax.broadcasted_iota(jnp.int32, array.shape, 0) + (array.shape[1] - array.shape[0])
    cols = lax.broadcasted_iota(jnp.int32, array.shape, 1)
    return jnp.where(cols <= rows, array, 0.0).astype(BF16)


def upper(array):
    rows = lax.broadcasted_iota(jnp.int32, array.shape, 0)
    cols = lax.broadcasted_iota(jnp.int32, array.shape, 1)
    return jnp.where(cols >= rows, array, 0.0).astype(BF16)


def intra_body(core, q, k, v, out):
    for h in range(2):
        cols = slice(h * DH, (h + 1) * DH)
        keys, values = k[:, cols], v[:, cols]
        top = lower(dot_nt(q[:HALF, cols], keys[:HALF]))
        out[:HALF, cols] = dot(top, values[:HALF])
        bottom = lower(dot_nt(q[HALF:, cols], keys))
        out[HALF:, cols] = dot(bottom, values)


def gather_state(core, base_own, base_other, side_own, side_other, weight):
    step = pl.program_id(0)
    own = base_own[...] + weight * side_own[...]
    other = base_other[...] + weight * side_other[...]
    return jnp.where(step < SIDE, own, other).astype(BF16)


def output_body(
    core, q, intra, out_grad, gain, base_own, base_other, side_own, side_other,
    output, prefix_half, stats, square_acc, product_acc,
):
    step = pl.program_id(0)

    @pl.when(step == 0)
    def _():
        square_acc[...] = jnp.zeros_like(square_acc)
        product_acc[...] = jnp.zeros_like(product_acc)

    weight = core[0].astype(F32)
    prefix = gather_state(core, base_own, base_other, side_own, side_other, weight)
    prefix_half[0] = prefix
    for h in range(2):
        cols = slice(h * DH, (h + 1) * DH)
        value = intra[:, cols] + dot(q[:, cols], prefix[cols, :])
        output[:, cols] = value
        scaled = out_grad[:, cols].astype(F32) * gain[:, cols]
        square_acc[...] += value * value
        product_acc[...] += scaled * value

    @pl.when(step == PAIRS - 1)
    def _():
        stats[0:1, :] = jnp.sum(square_acc[...].T, axis=0, keepdims=True)
        stats[1:2, :] = jnp.sum(product_acc[...].T, axis=0, keepdims=True)


def grad_body(core, q, output, out_grad, gain, s0, s1, s2, s3, grad_out, states, inverse, coeff):
    @pl.when(pl.program_id(0) == 0)
    def _():
        total = (s0[...] + s1[...]) + (s2[...] + s3[...])
        radius = jnp.sqrt(total[0:1, :] / WIDTH_ALL + epsilon)
        scale = total[1:2, :] / (WIDTH_ALL * radius * radius)
        inverse[...] = jnp.broadcast_to(1.0 / radius, (DH, BLOCK)).T
        coeff[...] = jnp.broadcast_to(scale, (DH, BLOCK)).T

    for h in range(2):
        cols = slice(h * DH, (h + 1) * DH)
        scaled = out_grad[:, cols].astype(F32) * gain[:, cols]
        grad = (scaled - output[:, cols] * coeff[...]) * inverse[...]
        grad_out[:, cols] = grad.astype(BF16)
    store_states(states, q[...], grad_out[...])


def middle_body(core, q, k, v, g, prefix_half, query_grad, key_part, value_part):
    for h in range(2):
        cols = slice(h * DH, (h + 1) * DH)
        queries, keys, values, grads = q[:, cols], k[:, cols], v[:, cols], g[:, cols]
        prefix = prefix_half[0, cols, :]
        for rows, seen in ((slice(0, HALF), slice(0, HALF)), (slice(HALF, BLOCK), slice(0, BLOCK))):
            mixing = lower(dot_nt(grads[rows], values[seen]))
            total = dot(mixing, keys[seen]) + dot_nt(grads[rows], prefix)
            query_grad[rows, cols] = total.astype(BF16)
        for rows, seen in ((slice(0, HALF), slice(0, BLOCK)), (slice(HALF, BLOCK), slice(HALF, BLOCK))):
            mixing = upper(dot_nt(values[rows], grads[seen]))
            key_part[rows, cols] = dot(mixing, queries[seen])
            scores = upper(dot_nt(keys[rows], queries[seen]))
            value_part[rows, cols] = dot(scores, grads[seen])


def last_body(
    core, k, v, key_part, value_part, base_own, base_other, side_own, side_other,
    key_grad, value_grad,
):
    weight = 1.0 - core[0].astype(F32)
    later = gather_state(core, base_own, base_other, side_own, side_other, weight)
    for h in range(2):
        cols = slice(h * DH, (h + 1) * DH)
        key_grad[:, cols] = (key_part[:, cols] + dot_nt(v[:, cols], later[cols, :])).astype(BF16)
        value_grad[:, cols] = (value_part[:, cols] + dot(k[:, cols], later[cols, :])).astype(BF16)


def scan_body(reverse, parts, out):
    state = jnp.zeros((SLICE, DH), F32)
    order = range(CHIPS - 1, -1, -1) if reverse else range(CHIPS)
    for place in order:
        out[place] = state
        state = state + parts[place]


def chip_scan(parts, reverse):
    return pl.pallas_call(
        functools.partial(scan_body, reverse),
        out_shape=shape((CHIPS, SLICE, DH), F32),
        compiler_params=pltpu.CompilerParams(vmem_limit_bytes=LIMIT),
        cost_estimate=pl.CostEstimate(flops=MIB, bytes_accessed=MIB, transcendentals=0),
    )(parts)


PARTNERS = [(i, i ^ 1) for i in range(2 * CHIPS)]
SAME_CORE = [[core + 2 * chip for chip in range(CHIPS)] for core in range(2)]


def exchange(parts):
    return lax.all_to_all(parts, "ctx", 0, 0, axis_index_groups=SAME_CORE, tiled=True)


def swap(part):
    return lax.ppermute(part, "ctx", PARTNERS)


def entering(states, reverse):
    own, other = states[0], states[1]
    side_own = swap(other)
    side_other = swap(own)
    chip = (own + side_own).reshape(CHIPS, SLICE, DH)
    base_own = exchange(chip_scan(exchange(chip), reverse)).reshape(ROWS, DH)
    base_other = swap(base_own)
    return base_own, base_other, side_own, side_other


def local(query_rows, key_rows, value_rows, out_grad, norm_gain):
    core = (lax.axis_index("ctx") % 2).astype(jnp.int32).reshape(1)
    gain = norm_gain.reshape(1, WIDTH)
    token, state = token_spec(), state_spec()
    halves = [half_spec(0), half_spec(1), half_spec(0), half_spec(1)]
    gain_spec = pl.BlockSpec((1, 2 * DH), columns)
    stats_spec = pl.BlockSpec((2, BLOCK), lambda step, core: (0, 0))
    lanes = pltpu.VMEM((BLOCK, DH), F32)
    stats_shape = shape((2, BLOCK), F32)

    states = call(
        local_state_body, [token, token], state, STATES, 2 * BLOCK * WIDTH * DH * 2, 5 * MIB
    )(core, key_rows, value_rows)
    bases = entering(states, False)
    intra = call(
        intra_body, [token] * 3, token, TOKENS_F32, 6 * BLOCK * BLOCK * WIDTH, 10 * MIB
    )(core, query_rows, key_rows, value_rows)
    output, prefix_half, stats = call(
        output_body,
        [token, token, token, gain_spec] + halves,
        [token, state, stats_spec],
        [TOKENS_F32, shape((2, ROWS, DH), BF16), stats_shape],
        2 * BLOCK * WIDTH * DH,
        14 * MIB,
        (lanes, lanes),
    )(core, query_rows, intra, out_grad, gain, *bases)
    others = [
        lax.ppermute(stats, "head", [(i, (i + hop) % 4) for i in range(4)]) for hop in (1, 2, 3)
    ]
    grad_out, grad_states = call(
        grad_body,
        [token, token, token, gain_spec] + [stats_spec] * 4,
        [token, state],
        [TOKENS_BF16, STATES],
        4 * BLOCK * WIDTH * DH,
        11 * MIB,
        (lanes, lanes),
    )(core, query_rows, output, out_grad, gain, stats, *others)
    laters = entering(grad_states, True)
    query_grad, key_part, value_part = call(
        middle_body,
        [token] * 4 + [state],
        [token] * 3,
        [TOKENS_BF16, TOKENS_F32, TOKENS_F32],
        10 * BLOCK * BLOCK * WIDTH,
        18 * MIB,
    )(core, query_rows, key_rows, value_rows, grad_out, prefix_half)
    key_grad, value_grad = call(
        last_body,
        [token] * 4 + halves,
        [token, token],
        [TOKENS_BF16, TOKENS_BF16],
        4 * BLOCK * WIDTH * DH,
        18 * MIB,
    )(core, key_rows, value_rows, key_part, value_part, *laters)
    return query_grad, key_grad, value_grad


def solution(mesh):
    in_specs = (P("ctx", "head"), P("ctx", "head"), P("ctx", "head"), P("ctx", "head"), P("head"))
    out_specs = (P("ctx", "head"), P("ctx", "head"), P("ctx", "head"))
    return jax.shard_map(local, mesh=mesh, in_specs=in_specs, out_specs=out_specs, check_vma=False)
```

```python
import functools

import jax
import jax.numpy as jnp
from jax import lax
from jax.experimental import pallas as pl
from jax.experimental.pallas import tpu as pltpu
from jax.sharding import PartitionSpec as P

DH = 128
BLOCK = 512
HALF = 256
WIDTH = 2048
SIDE = WIDTH // 2
WIDTH_ALL = 8192
HEADS_SIDE = SIDE // DH
PAIRS_SIDE = HEADS_SIDE // 2
ROWS = HEADS_SIDE * DH
CHIPS = 16
SLICE = ROWS // CHIPS
MIB = 1024 * 1024

epsilon = 1e-06

F32 = jnp.float32
BF16 = jnp.bfloat16

VMEM = pl.BlockSpec(memory_space=pltpu.VMEM)
SMEM = pl.BlockSpec(memory_space=pltpu.SMEM)
HBM = pl.BlockSpec(memory_space=pltpu.HBM)


def hbm(dims, kind):
    return pltpu.HBM(dims, kind)


SIDE_F32 = jax.ShapeDtypeStruct((BLOCK, SIDE), F32)
SIDE_BF16 = jax.ShapeDtypeStruct((BLOCK, SIDE), BF16)
STATE = jax.ShapeDtypeStruct((ROWS, DH), F32)
STATE_HALF = jax.ShapeDtypeStruct((ROWS, DH), BF16)
LANES = jax.ShapeDtypeStruct((BLOCK, DH), F32)
STATS = jax.ShapeDtypeStruct((2, BLOCK), F32)
WHOLE = hbm((BLOCK, WIDTH), BF16)
FAR_F32 = hbm((BLOCK, SIDE), F32)
FAR_BF16 = hbm((BLOCK, SIDE), BF16)
BUFFER_F32 = pltpu.VMEM((BLOCK, SIDE), F32)
FIRST_BUFFER = pltpu.VMEM((HEADS_SIDE * HALF, HALF), BF16)
LAST_BUFFER = pltpu.VMEM((HEADS_SIDE * BLOCK, HALF), BF16)
BUFFER_BF16 = pltpu.VMEM((BLOCK, SIDE), BF16)


def copies_of(pairs, sems):
    copies = []
    for place, (source, target) in enumerate(pairs):
        copy = pltpu.make_async_copy(source, target, sems.at[place])
        copy.start()
        copies.append(copy)
    return copies


def wait(copies):
    for copy in copies:
        copy.wait()


def call(name, body, in_specs, out_specs, out_shape, flops, moved, scratch=(), aliases=None):
    kernel = pl.pallas_call(
        body,
        in_specs=in_specs,
        out_specs=out_specs,
        out_shape=out_shape,
        scratch_shapes=list(scratch),
        input_output_aliases=aliases or {},
        compiler_params=pltpu.CompilerParams(vmem_limit_bytes=16 * MIB),
        cost_estimate=pl.CostEstimate(flops=flops, bytes_accessed=moved, transcendentals=0),
        name=name,
    )

    def run(*arrays):
        return kernel(
            *(
                pltpu.with_memory_space_constraint(array, pltpu.HBM) if spec is HBM else array
                for spec, array in zip(in_specs, arrays)
            )
        )

    return run


def dot(a, b):
    return lax.dot_general(a, b, (((1,), (0,)), ((), ())), preferred_element_type=F32)


def dot_nt(a, b):
    return lax.dot_general(a, b, (((1,), (1,)), ((), ())), preferred_element_type=F32)


def dot_tn(a, b):
    return lax.dot_general(a, b, (((0,), (0,)), ((), ())), preferred_element_type=F32)


def pair_columns(pair):
    return slice(pair * 2 * DH, (pair + 1) * 2 * DH)


def head_columns(head):
    return slice(head * DH, (head + 1) * DH)


def diagonal(states, pair):
    first = states[2 * pair * DH : (2 * pair + 1) * DH, :]
    second = states[(2 * pair + 1) * DH : (2 * pair + 2) * DH, :]
    zero = jnp.zeros_like(first)
    return jnp.concatenate(
        [jnp.concatenate([first, zero], axis=1), jnp.concatenate([zero, second], axis=1)], axis=0
    )


def store_states(out, pair, a, b):
    both = dot_tn(a, b)
    out[2 * pair * DH : (2 * pair + 1) * DH, :] = both[:DH, :DH]
    out[(2 * pair + 1) * DH : (2 * pair + 2) * DH, :] = both[DH:, DH:]


def seen_keys():
    rows = lax.broadcasted_iota(jnp.int32, (HALF, HALF), 0)
    cols = lax.broadcasted_iota(jnp.int32, (HALF, HALF), 1)
    return cols <= rows


def seen_queries():
    rows = lax.broadcasted_iota(jnp.int32, (HALF, HALF), 0)
    cols = lax.broadcasted_iota(jnp.int32, (HALF, HALF), 1)
    return cols >= rows


def keep(mask, array):
    return jnp.where(mask, array, 0.0).astype(BF16)


TOP = slice(0, HALF)
BOTTOM = slice(HALF, BLOCK)


def by_keys(mask, queries, keys):
    first = dot_nt(queries, keys[TOP])
    last = dot_nt(queries[BOTTOM], keys[BOTTOM])
    first = jnp.concatenate([keep(mask, first[TOP]), first[BOTTOM].astype(BF16)], axis=0)
    return first, keep(mask, last)


def by_queries(mask, keys, queries):
    first = dot_nt(keys[TOP], queries[TOP])
    last = dot_nt(keys, queries[BOTTOM])
    last = jnp.concatenate([last[TOP].astype(BF16), keep(mask, last[BOTTOM])], axis=0)
    return keep(mask, first), last


def side_start(core, side):
    half = core[0] if side == 0 else 1 - core[0]
    return pl.multiple_of(half * SIDE, SIDE)


def pair_window(core, side, pair):
    return pl.ds(pl.multiple_of(side_start(core, side) + pair * 2 * DH, 2 * DH), 2 * DH)


def head_window(core, side, head):
    return pl.ds(pl.multiple_of(side_start(core, side) + head * DH, DH), DH)


PAIRS = range(PAIRS_SIDE)


def local_state_body(side, core, k_all, v_all, out, k, v, sems):
    copies = copies_of(
        [
            (source.at[:, pair_window(core, side, pair)], target.at[:, pair_columns(pair)])
            for pair in PAIRS
            for source, target in ((k_all, k), (v_all, v))
        ],
        sems,
    )
    for pair in PAIRS:
        wait(copies[2 * pair : 2 * pair + 2])
        store_states(out, pair, k[:, pair_columns(pair)], v[:, pair_columns(pair)])


def local_state(side, core, keys, values):
    return call(
        f"state{side}",
        functools.partial(local_state_body, side),
        [SMEM, HBM, HBM],
        VMEM,
        STATE,
        2 * BLOCK * SIDE * DH,
        2 * MIB,
        [BUFFER_BF16, BUFFER_BF16, pltpu.SemaphoreType.DMA((2 * PAIRS_SIDE,))],
    )(core, keys, values)


def first_rows(pair):
    return pl.ds(2 * pair * HALF, 2 * HALF)


def last_rows(pair):
    return pl.ds(2 * pair * BLOCK, 2 * BLOCK)


def intra_body(
    side, core, q_all, k_all, v_all, far, first_far, last_far, q, k, v, out, first, last, sems, out_sems
):
    before, behind = seen_keys(), seen_queries()
    copies = copies_of(
        [
            (source.at[:, pair_window(core, side, pair)], target.at[:, pair_columns(pair)])
            for pair in PAIRS
            for source, target in ((q_all, q), (k_all, k), (v_all, v))
        ],
        sems,
    )
    results = []
    for pair in PAIRS:
        wait(copies[3 * pair : 3 * pair + 3])
        for head in (2 * pair, 2 * pair + 1):
            cols = head_columns(head)
            queries, keys, values = q[:, cols], k[:, cols], v[:, cols]
            scores0, scores1 = by_keys(before, queries, keys)
            first[pl.ds(head * HALF, HALF), :], last[pl.ds(head * BLOCK, BLOCK), :] = by_queries(
                behind, keys, queries
            )
            total = dot(scores0, values[TOP])
            out[TOP, cols] = total[TOP]
            out[BOTTOM, cols] = total[BOTTOM] + dot(scores1, values[BOTTOM])
        cols = pair_columns(pair)
        results += copies_of(
            [
                (out.at[:, cols], far.at[:, cols]),
                (first.at[first_rows(pair)], first_far.at[first_rows(pair)]),
                (last.at[last_rows(pair)], last_far.at[last_rows(pair)]),
            ],
            out_sems.at[pl.ds(3 * pair, 3)],
        )
    wait(results)


def intra_output(side, core, queries, keys, values):
    return call(
        f"intra{side}",
        functools.partial(intra_body, side),
        [SMEM, HBM, HBM, HBM],
        [HBM] * 3,
        [FAR_F32, hbm((HEADS_SIDE * HALF, HALF), BF16), hbm((HEADS_SIDE * BLOCK, HALF), BF16)],
        5 * BLOCK * BLOCK * SIDE,
        8 * MIB,
        [BUFFER_BF16] * 3
        + [BUFFER_F32, FIRST_BUFFER, LAST_BUFFER]
        + [pltpu.SemaphoreType.DMA((3 * PAIRS_SIDE,))] * 2,
    )(core, queries, keys, values)


def output_body(side, core, *refs):
    if side == 0:
        q_all, o_all, intra, intra1, gain, base, near = refs[:7]
        q, o, output, prefix_half, squares, products, q1, o1, near_output1, sems = refs[7:]
        copies = [
            (source.at[:, window], target.at[:, pair_columns(pair)])
            for pair in PAIRS
            for source, target, window in (
                (q_all, q, pair_window(core, 0, pair)),
                (intra, output, pair_columns(pair)),
                (o_all, o, pair_window(core, 0, pair)),
            )
        ]
        other = pl.ds(side_start(core, 1), SIDE)
        copies += [(q_all.at[:, other], q1), (o_all.at[:, other], o1), (intra1, near_output1)]
        copies = copies_of(copies, sems)
    else:
        q, o, intra, gain, base, near, squares_in, products_in = refs[:8]
        output, prefix_half, stats = refs[8:]
    weight = core[0].astype(F32)
    gains = gain[:, pl.ds(side_start(core, side), SIDE)]
    prefix_half[...] = (base[...] + weight * near[...]).astype(BF16)
    parts = (slice(0, HALF), slice(HALF, BLOCK))
    if side == 0:
        square_sums = [jnp.zeros((HALF, DH), F32) for rows in parts]
        product_sums = [jnp.zeros((HALF, DH), F32) for rows in parts]
    else:
        square_sums = [squares_in[rows, :] for rows in parts]
        product_sums = [products_in[rows, :] for rows in parts]
    for pair in PAIRS:
        cols = pair_columns(pair)
        if side == 0:
            wait(copies[3 * pair : 3 * pair + 3])
        states = diagonal(prefix_half, pair)
        for part, rows in enumerate(parts):
            start = output if side == 0 else intra
            value = start[rows, cols] + dot(q[rows, cols], states)
            output[rows, cols] = value
            terms = o[rows, cols].astype(F32) * gains[:, cols] * value
            value = value * value
            square_sums[part] = square_sums[part] + (value[:, :DH] + value[:, DH:])
            product_sums[part] = product_sums[part] + (terms[:, :DH] + terms[:, DH:])
    for part, rows in enumerate(parts):
        if side == 0:
            squares[rows, :] = square_sums[part]
            products[rows, :] = product_sums[part]
        else:
            stats[0:1, rows] = jnp.sum(square_sums[part].T, axis=0, keepdims=True)
            stats[1:2, rows] = jnp.sum(product_sums[part].T, axis=0, keepdims=True)
    if side == 0:
        wait(copies[3 * PAIRS_SIDE :])


def output_own(core, queries, out_grad, intra, intra1, gain, base, near):
    return call(
        "output0",
        functools.partial(output_body, 0),
        [SMEM] + [HBM] * 4 + [VMEM] * 3,
        [VMEM] * 9,
        [SIDE_BF16, SIDE_BF16, SIDE_F32, STATE_HALF, LANES, LANES, SIDE_BF16, SIDE_BF16, SIDE_F32],
        2 * BLOCK * SIDE * DH,
        8 * MIB,
        [pltpu.SemaphoreType.DMA((3 * PAIRS_SIDE + 3,))],
    )(core, queries, out_grad, intra, intra1, gain, base, near)


def output_other(core, q, o, intra, gain, base, near, squares, products):
    return call(
        "output1",
        functools.partial(output_body, 1),
        [SMEM] + [VMEM] * 8,
        [VMEM] * 3,
        [SIDE_F32, STATE_HALF, STATS],
        2 * BLOCK * SIDE * DH,
        MIB,
    )(core, q, o, intra, gain, base, near, squares, products)


def grad_body(side, core, q, output, o, gain, s0, s1, s2, s3, far, states, grad_out, sems):
    total = (s0[...] + s1[...]) + (s2[...] + s3[...])
    mean_square = total[0:1, :] / WIDTH_ALL + epsilon
    radius = jnp.sqrt(mean_square)
    scale = total[1:2, :] / (WIDTH_ALL * radius * radius)
    inverse = jnp.broadcast_to(1.0 / radius, (DH, BLOCK)).T
    coeff = jnp.broadcast_to(scale, (DH, BLOCK)).T
    gains = gain[:, pl.ds(side_start(core, side), SIDE)]
    for rows in range(0, BLOCK, DH):
        rows = slice(rows, rows + DH)
        inverse_rows, coeff_rows = inverse[rows, :], coeff[rows, :]
        for head in range(HEADS_SIDE):
            cols = head_columns(head)
            scaled = o[rows, cols].astype(F32) * gains[:, cols]
            grad = (scaled - output[rows, cols] * coeff_rows) * inverse_rows
            grad_out[rows, cols] = grad.astype(BF16)
    copies = copies_of([(grad_out, far)], sems)
    for pair in PAIRS:
        store_states(states, pair, q[:, pair_columns(pair)], grad_out[:, pair_columns(pair)])
    wait(copies)


def local_grad(side, core, q, output, o, gain, stats):
    return call(
        f"grad{side}",
        functools.partial(grad_body, side),
        [SMEM] + [VMEM] * 8,
        [HBM, VMEM],
        [FAR_BF16, STATE],
        2 * BLOCK * SIDE * DH,
        MIB,
        [BUFFER_BF16, pltpu.SemaphoreType.DMA((1,))],
    )(core, q, output, o, gain, *stats)


def query_body(side, core, k_all, v_all, grad_out, prefix, *refs):
    query_grad, k, v, g, result, sems, out_sems = refs[-7:]
    before = seen_keys()
    copies = copies_of(
        [
            (source.at[:, window], target.at[:, pair_columns(pair)])
            for pair in PAIRS
            for source, target, window in (
                (k_all, k, pair_window(core, side, pair)),
                (v_all, v, pair_window(core, side, pair)),
                (grad_out, g, pair_columns(pair)),
            )
        ],
        sems,
    )
    results = []
    for pair in PAIRS:
        wait(copies[3 * pair : 3 * pair + 3])
        across = dot_nt(g[:, pair_columns(pair)], diagonal(prefix, pair))
        for h in range(2):
            cols = head_columns(2 * pair + h)
            part = across[:, h * DH : (h + 1) * DH]
            mixing0, mixing1 = by_keys(before, g[:, cols], v[:, cols])
            total = part + dot(mixing0, k[TOP, cols])
            result[TOP, cols] = total[TOP].astype(BF16)
            result[BOTTOM, cols] = (total[BOTTOM] + dot(mixing1, k[BOTTOM, cols])).astype(BF16)
        results += copies_of(
            [(result.at[:, pair_columns(pair)], query_grad.at[:, pair_window(core, side, pair)])],
            out_sems.at[pl.ds(pair, 1)],
        )
    wait(results)


def query_gradient(side, core, keys, values, g, prefix, result=()):
    return call(
        f"query{side}",
        functools.partial(query_body, side),
        [SMEM, HBM, HBM, HBM, VMEM] + [HBM] * len(result),
        HBM,
        WHOLE,
        4 * BLOCK * BLOCK * SIDE,
        4 * MIB,
        [BUFFER_BF16] * 4
        + [pltpu.SemaphoreType.DMA((3 * PAIRS_SIDE,)), pltpu.SemaphoreType.DMA((PAIRS_SIDE,))],
        {5 + i: i for i in range(len(result))},
    )(core, keys, values, g, prefix, *result)


def part_body(side, core, q_all, v_all, g_far, first_far, last_far, key_far, value_far, *refs):
    q, v, g, first, last, key_part, value_part, sems, out_sems = refs
    behind = seen_queries()
    copies = copies_of(
        [
            (source.at[:, window], target.at[:, pair_columns(pair)])
            for pair in PAIRS
            for source, target, window in (
                (q_all, q, pair_window(core, side, pair)),
                (v_all, v, pair_window(core, side, pair)),
                (g_far, g, pair_columns(pair)),
            )
        ]
        + [
            (source.at[rows(pair)], target.at[rows(pair)])
            for pair in PAIRS
            for source, target, rows in ((first_far, first, first_rows), (last_far, last, last_rows))
        ],
        sems,
    )
    results = []
    for pair in PAIRS:
        wait(copies[3 * pair : 3 * pair + 3])
        wait(copies[3 * PAIRS_SIDE + 2 * pair : 3 * PAIRS_SIDE + 2 * pair + 2])
        for head in (2 * pair, 2 * pair + 1):
            cols = head_columns(head)
            mixing0, mixing1 = by_queries(behind, v[:, cols], g[:, cols])
            total = dot(last[pl.ds(head * BLOCK, BLOCK), :], g[BOTTOM, cols])
            value_part[TOP, cols] = total[TOP] + dot(first[pl.ds(head * HALF, HALF), :], g[TOP, cols])
            value_part[BOTTOM, cols] = total[BOTTOM]
            total = dot(mixing1, q[BOTTOM, cols])
            key_part[TOP, cols] = total[TOP] + dot(mixing0, q[TOP, cols])
            key_part[BOTTOM, cols] = total[BOTTOM]
        cols = pair_columns(pair)
        results += copies_of(
            [(key_part.at[:, cols], key_far.at[:, cols]), (value_part.at[:, cols], value_far.at[:, cols])],
            out_sems.at[pl.ds(2 * pair, 2)],
        )
    wait(results)


def key_value_parts(side, core, queries, values, g, turned):
    return call(
        f"part{side}",
        functools.partial(part_body, side),
        [SMEM] + [HBM] * 5,
        [HBM] * 2,
        [FAR_F32, FAR_F32],
        5 * BLOCK * BLOCK * SIDE,
        10 * MIB,
        [BUFFER_BF16] * 3
        + [FIRST_BUFFER, LAST_BUFFER]
        + [BUFFER_F32] * 2
        + [pltpu.SemaphoreType.DMA((5 * PAIRS_SIDE,)), pltpu.SemaphoreType.DMA((2 * PAIRS_SIDE,))],
    )(core, queries, values, g, *turned)


def last_body(side, core, *refs):
    if side == 0:
        k_all, v_all, key_far, value_far, key_far1, value_far1, base, near = refs[:8]
        key_grad, value_grad, k1, v1, key_part1, value_part1 = refs[8:14]
        k, v, key_part, value_part, key_half, value_half, sems, out_sems = refs[14:]
        other = pl.ds(side_start(core, 1), SIDE)
        copies = [
            (source.at[:, window], target.at[:, pair_columns(pair)])
            for pair in PAIRS
            for source, target, window in (
                (k_all, k, pair_window(core, 0, pair)),
                (v_all, v, pair_window(core, 0, pair)),
                (key_far, key_part, pair_columns(pair)),
                (value_far, value_part, pair_columns(pair)),
            )
        ]
        copies += [
            (k_all.at[:, other], k1),
            (v_all.at[:, other], v1),
            (key_far1, key_part1),
            (value_far1, value_part1),
        ]
        copies = copies_of(copies, sems)
    else:
        k, v, key_part, value_part, base, near = refs[:6]
        key_grad, value_grad, key_half, value_half, out_sems = refs[8:]
    weight = 1.0 - core[0].astype(F32)
    later = (base[...] + weight * near[...]).astype(BF16)
    results = []
    for pair in PAIRS:
        cols = pair_columns(pair)
        if side == 0:
            wait(copies[4 * pair : 4 * pair + 4])
        states = diagonal(later, pair)
        key_half[:, cols] = (key_part[:, cols] + dot_nt(v[:, cols], states)).astype(BF16)
        value_half[:, cols] = (value_part[:, cols] + dot(k[:, cols], states)).astype(BF16)
        window = pair_window(core, side, pair)
        results += copies_of(
            [(key_half.at[:, cols], key_grad.at[:, window]), (value_half.at[:, cols], value_grad.at[:, window])],
            out_sems.at[pl.ds(2 * pair, 2)],
        )
    wait(results)
    if side == 0:
        wait(copies[4 * PAIRS_SIDE :])


def last_own(core, keys, values, part, part1, base, near):
    return call(
        "last0",
        functools.partial(last_body, 0),
        [SMEM] + [HBM] * 6 + [VMEM] * 2,
        [HBM, HBM] + [VMEM] * 4,
        [WHOLE, WHOLE, SIDE_BF16, SIDE_BF16, SIDE_F32, SIDE_F32],
        4 * BLOCK * SIDE * DH,
        12 * MIB,
        [BUFFER_BF16, BUFFER_BF16, BUFFER_F32, BUFFER_F32, BUFFER_BF16, BUFFER_BF16]
        + [pltpu.SemaphoreType.DMA((4 * PAIRS_SIDE + 4,)), pltpu.SemaphoreType.DMA((2 * PAIRS_SIDE,))],
    )(core, keys, values, *part, *part1, base, near)


def last_other(core, k, v, key_part, value_part, base, near, key_grad, value_grad):
    return call(
        "last1",
        functools.partial(last_body, 1),
        [SMEM] + [VMEM] * 6 + [HBM] * 2,
        [HBM, HBM],
        [WHOLE, WHOLE],
        4 * BLOCK * SIDE * DH,
        2 * MIB,
        [BUFFER_BF16, BUFFER_BF16, pltpu.SemaphoreType.DMA((2 * PAIRS_SIDE,))],
        {7: 0, 8: 1},
    )(core, k, v, key_part, value_part, base, near, key_grad, value_grad)


def scan_body(reverse, parts, far, out, sems):
    state = jnp.zeros((SLICE, DH), F32)
    order = range(CHIPS - 1, -1, -1) if reverse else range(CHIPS)
    for place in order:
        out[place] = state
        state = state + parts[place]
    wait(copies_of([(out, far)], sems))


def chip_scan(parts, reverse):
    return call(
        f"scan{int(reverse)}",
        functools.partial(scan_body, reverse),
        [VMEM],
        HBM,
        hbm((CHIPS, SLICE, DH), F32),
        MIB,
        MIB,
        [pltpu.VMEM((CHIPS, SLICE, DH), F32), pltpu.SemaphoreType.DMA((1,))],
    )(parts)


PARTNERS = [(i, i ^ 1) for i in range(2 * CHIPS)]
SAME_CORE = [[core + 2 * chip for chip in range(CHIPS)] for core in range(2)]


def exchange(parts):
    return lax.all_to_all(parts, "ctx", 0, 0, axis_index_groups=SAME_CORE, tiled=True)


def swap(part):
    return lax.ppermute(part, "ctx", PARTNERS)


def along_heads(stats):
    hops = (1, 2, 3)
    return [lax.ppermute(stats, "head", [(i, (i + hop) % 4) for i in range(4)]) for hop in hops]


def after(value, *done):
    return lax.optimization_barrier((value,) + done)[0]


def local(query_rows, key_rows, value_rows, out_grad, norm_gain):
    core = (lax.axis_index("ctx") % 2).astype(jnp.int32).reshape(1)
    return device(core, query_rows, key_rows, value_rows, out_grad, norm_gain)


def device(core, query_rows, key_rows, value_rows, out_grad, norm_gain):
    gain = norm_gain.reshape(1, WIDTH)
    everything = (query_rows, key_rows, value_rows)

    state1 = local_state(1, core, key_rows, value_rows)
    near0 = swap(state1)
    state0 = local_state(0, core, key_rows, value_rows)
    parts = exchange((state0 + near0).reshape(CHIPS, SLICE, DH))
    near1 = swap(state0)
    intra0, *turned0 = intra_output(0, core, *everything)
    sums = chip_scan(after(parts, intra0), False)
    base0 = exchange(sums).reshape(ROWS, DH)
    intra1, *turned1 = intra_output(1, core, *everything)
    base0 = after(base0, intra1)
    base1 = swap(base0)
    q0, o0, output0, prefix0, squares, products, q1, o1, intra1 = output_own(
        core, query_rows, out_grad, intra0, intra1, gain, base0, near0
    )
    output1, prefix1, stats = output_other(
        core, q1, o1, intra1, gain, base1, near1, squares, products
    )
    stats = [stats] + along_heads(stats)

    g1, state1 = local_grad(1, core, q1, output1, o1, gain, stats)
    near0 = swap(state1)
    g0, state0 = local_grad(0, core, q0, output0, o0, gain, stats)
    parts = exchange((state0 + near0).reshape(CHIPS, SLICE, DH))
    near1 = swap(state0)
    part0 = key_value_parts(0, core, query_rows, value_rows, g0, turned0)
    query_grad = query_gradient(0, core, key_rows, value_rows, g0, prefix0)
    sums = chip_scan(after(parts, *part0, query_grad), True)
    base0 = exchange(sums).reshape(ROWS, DH)
    part1 = key_value_parts(1, core, query_rows, value_rows, g1, turned1)
    query_grad = query_gradient(1, core, key_rows, value_rows, g1, prefix1, (query_grad,))
    base0 = after(base0, *part1, query_grad)
    base1 = swap(base0)
    key_grad, value_grad, *rest = last_own(core, key_rows, value_rows, part0, part1, base0, near0)
    key_grad, value_grad = last_other(core, *rest, base1, near1, key_grad, value_grad)
    return query_grad, key_grad, value_grad


def solution(mesh):
    in_specs = (P("ctx", "head"), P("ctx", "head"), P("ctx", "head"), P("ctx", "head"), P("head"))
    out_specs = (P("ctx", "head"), P("ctx", "head"), P("ctx", "head"))
    return jax.shard_map(local, mesh=mesh, in_specs=in_specs, out_specs=out_specs, check_vma=False)
```

```python
import functools

import jax
import jax.numpy as jnp
from jax import lax
from jax.experimental import pallas as pl
from jax.experimental.pallas import tpu as pltpu
from jax.sharding import PartitionSpec as P

DH = 128
BLOCK = 512
HALF = 256
WIDTH = 2048
SIDE = WIDTH // 2
WIDTH_ALL = 8192
HEADS_SIDE = SIDE // DH
PAIRS_SIDE = HEADS_SIDE // 2
ROWS = HEADS_SIDE * DH
CHIPS = 16
SLICE = ROWS // CHIPS
MIB = 1024 * 1024

epsilon = 1e-06

F32 = jnp.float32
BF16 = jnp.bfloat16

VMEM = pl.BlockSpec(memory_space=pltpu.VMEM)
SMEM = pl.BlockSpec(memory_space=pltpu.SMEM)
HBM = pl.BlockSpec(memory_space=pltpu.HBM)


def hbm(dims, kind):
    return pltpu.HBM(dims, kind)


SIDE_F32 = jax.ShapeDtypeStruct((BLOCK, SIDE), F32)
SIDE_BF16 = jax.ShapeDtypeStruct((BLOCK, SIDE), BF16)
STATE = jax.ShapeDtypeStruct((ROWS, DH), F32)
STATE_HALF = jax.ShapeDtypeStruct((ROWS, DH), BF16)
LANES = jax.ShapeDtypeStruct((BLOCK, DH), F32)
STATS = jax.ShapeDtypeStruct((2, BLOCK), F32)
WHOLE = hbm((BLOCK, WIDTH), BF16)
FAR_F32 = hbm((BLOCK, SIDE), F32)
FAR_BF16 = hbm((BLOCK, SIDE), BF16)
BUFFER_F32 = pltpu.VMEM((BLOCK, SIDE), F32)
FIRST_BUFFER = pltpu.VMEM((HEADS_SIDE * HALF, HALF), BF16)
LAST_BUFFER = pltpu.VMEM((HEADS_SIDE * BLOCK, HALF), BF16)
BUFFER_BF16 = pltpu.VMEM((BLOCK, SIDE), BF16)


def copies_of(pairs, sems):
    copies = []
    for place, (source, target) in enumerate(pairs):
        copy = pltpu.make_async_copy(source, target, sems.at[place])
        copy.start()
        copies.append(copy)
    return copies


def wait(copies):
    for copy in copies:
        copy.wait()


def call(name, body, in_specs, out_specs, out_shape, flops, moved, scratch=(), aliases=None):
    kernel = pl.pallas_call(
        body,
        in_specs=in_specs,
        out_specs=out_specs,
        out_shape=out_shape,
        scratch_shapes=list(scratch),
        input_output_aliases=aliases or {},
        compiler_params=pltpu.CompilerParams(vmem_limit_bytes=20 * MIB),
        cost_estimate=pl.CostEstimate(flops=flops, bytes_accessed=moved, transcendentals=0),
        name=name,
    )

    def run(*arrays):
        return kernel(
            *(
                pltpu.with_memory_space_constraint(array, pltpu.HBM) if spec is HBM else array
                for spec, array in zip(in_specs, arrays)
            )
        )

    return run


def dot(a, b):
    return lax.dot_general(a, b, (((1,), (0,)), ((), ())), preferred_element_type=F32)


def dot_nt(a, b):
    return lax.dot_general(a, b, (((1,), (1,)), ((), ())), preferred_element_type=F32)


def dot_tn(a, b):
    return lax.dot_general(a, b, (((0,), (0,)), ((), ())), preferred_element_type=F32)


def pair_columns(pair):
    return slice(pair * 2 * DH, (pair + 1) * 2 * DH)


def head_columns(head):
    return slice(head * DH, (head + 1) * DH)


def diagonal(states, pair):
    first = states[2 * pair * DH : (2 * pair + 1) * DH, :]
    second = states[(2 * pair + 1) * DH : (2 * pair + 2) * DH, :]
    zero = jnp.zeros_like(first)
    return jnp.concatenate(
        [jnp.concatenate([first, zero], axis=1), jnp.concatenate([zero, second], axis=1)], axis=0
    )


def store_states(out, pair, a, b):
    both = dot_tn(a, b)
    out[2 * pair * DH : (2 * pair + 1) * DH, :] = both[:DH, :DH]
    out[(2 * pair + 1) * DH : (2 * pair + 2) * DH, :] = both[DH:, DH:]


def seen_keys():
    rows = lax.broadcasted_iota(jnp.int32, (HALF, HALF), 0)
    cols = lax.broadcasted_iota(jnp.int32, (HALF, HALF), 1)
    return cols <= rows


def seen_queries():
    rows = lax.broadcasted_iota(jnp.int32, (HALF, HALF), 0)
    cols = lax.broadcasted_iota(jnp.int32, (HALF, HALF), 1)
    return cols >= rows


def keep(mask, array):
    return jnp.where(mask, array, 0.0).astype(BF16)


TOP = slice(0, HALF)
BOTTOM = slice(HALF, BLOCK)


def by_keys(mask, queries, keys):
    first = dot_nt(queries, keys[TOP])
    last = dot_nt(queries[BOTTOM], keys[BOTTOM])
    first = jnp.concatenate([keep(mask, first[TOP]), first[BOTTOM].astype(BF16)], axis=0)
    return first, keep(mask, last)


def by_queries(mask, keys, queries):
    first = dot_nt(keys[TOP], queries[TOP])
    last = dot_nt(keys, queries[BOTTOM])
    last = jnp.concatenate([last[TOP].astype(BF16), keep(mask, last[BOTTOM])], axis=0)
    return keep(mask, first), last


def side_start(core, side):
    half = core[0] if side == 0 else 1 - core[0]
    return pl.multiple_of(half * SIDE, SIDE)


def pair_window(core, side, pair):
    return pl.ds(pl.multiple_of(side_start(core, side) + pair * 2 * DH, 2 * DH), 2 * DH)


def head_window(core, side, head):
    return pl.ds(pl.multiple_of(side_start(core, side) + head * DH, DH), DH)


PAIRS = range(PAIRS_SIDE)


def local_state_body(side, core, k_all, v_all, out, k, v, sems):
    copies = copies_of(
        [
            (source.at[:, pair_window(core, side, pair)], target.at[:, pair_columns(pair)])
            for pair in PAIRS
            for source, target in ((k_all, k), (v_all, v))
        ],
        sems,
    )
    for pair in PAIRS:
        wait(copies[2 * pair : 2 * pair + 2])
        store_states(out, pair, k[:, pair_columns(pair)], v[:, pair_columns(pair)])


def local_state(side, core, keys, values):
    return call(
        f"state{side}",
        functools.partial(local_state_body, side),
        [SMEM, HBM, HBM],
        VMEM,
        STATE,
        2 * BLOCK * SIDE * DH,
        2 * MIB,
        [BUFFER_BF16, BUFFER_BF16, pltpu.SemaphoreType.DMA((2 * PAIRS_SIDE,))],
    )(core, keys, values)


def first_rows(pair):
    return pl.ds(2 * pair * HALF, 2 * HALF)


def last_rows(pair):
    return pl.ds(2 * pair * BLOCK, 2 * BLOCK)


def intra_body(
    side, core, q_all, k_all, v_all, far, first_far, last_far, q, k, v, out, first, last, sems, out_sems
):
    before, behind = seen_keys(), seen_queries()
    copies = copies_of(
        [
            (source.at[:, pair_window(core, side, pair)], target.at[:, pair_columns(pair)])
            for pair in PAIRS
            for source, target in ((q_all, q), (k_all, k), (v_all, v))
        ],
        sems,
    )
    results = []
    for pair in PAIRS:
        wait(copies[3 * pair : 3 * pair + 3])
        for head in (2 * pair, 2 * pair + 1):
            cols = head_columns(head)
            queries, keys, values = q[:, cols], k[:, cols], v[:, cols]
            scores0, scores1 = by_keys(before, queries, keys)
            first[pl.ds(head * HALF, HALF), :], last[pl.ds(head * BLOCK, BLOCK), :] = by_queries(
                behind, keys, queries
            )
            total = dot(scores0, values[TOP])
            out[TOP, cols] = total[TOP]
            out[BOTTOM, cols] = total[BOTTOM] + dot(scores1, values[BOTTOM])
        cols = pair_columns(pair)
        results += copies_of(
            [
                (out.at[:, cols], far.at[:, cols]),
                (first.at[first_rows(pair)], first_far.at[first_rows(pair)]),
                (last.at[last_rows(pair)], last_far.at[last_rows(pair)]),
            ],
            out_sems.at[pl.ds(3 * pair, 3)],
        )
    wait(results)


def intra_output(side, core, queries, keys, values):
    return call(
        f"intra{side}",
        functools.partial(intra_body, side),
        [SMEM, HBM, HBM, HBM],
        [HBM] * 3,
        [FAR_F32, hbm((HEADS_SIDE * HALF, HALF), BF16), hbm((HEADS_SIDE * BLOCK, HALF), BF16)],
        5 * BLOCK * BLOCK * SIDE,
        8 * MIB,
        [BUFFER_BF16] * 3
        + [BUFFER_F32, FIRST_BUFFER, LAST_BUFFER]
        + [pltpu.SemaphoreType.DMA((3 * PAIRS_SIDE,))] * 2,
    )(core, queries, keys, values)


def output_body(side, core, *refs):
    if side == 0:
        q_all, o_all, intra, intra1, gain, base, near = refs[:7]
        q, o, output, prefix_half, squares, products, q1, o1, near_output1, sems = refs[7:]
        copies = [
            (source.at[:, window], target.at[:, pair_columns(pair)])
            for pair in PAIRS
            for source, target, window in (
                (q_all, q, pair_window(core, 0, pair)),
                (intra, output, pair_columns(pair)),
                (o_all, o, pair_window(core, 0, pair)),
            )
        ]
        other = pl.ds(side_start(core, 1), SIDE)
        copies += [(q_all.at[:, other], q1), (o_all.at[:, other], o1), (intra1, near_output1)]
        copies = copies_of(copies, sems)
    else:
        q, o, intra, gain, base, near, squares_in, products_in = refs[:8]
        output, prefix_half, stats = refs[8:]
    weight = core[0].astype(F32)
    gains = gain[:, pl.ds(side_start(core, side), SIDE)]
    prefix_half[...] = (base[...] + weight * near[...]).astype(BF16)
    parts = (slice(0, HALF), slice(HALF, BLOCK))
    if side == 0:
        square_sums = [jnp.zeros((HALF, DH), F32) for rows in parts]
        product_sums = [jnp.zeros((HALF, DH), F32) for rows in parts]
    else:
        square_sums = [squares_in[rows, :] for rows in parts]
        product_sums = [products_in[rows, :] for rows in parts]
    for pair in PAIRS:
        cols = pair_columns(pair)
        if side == 0:
            wait(copies[3 * pair : 3 * pair + 3])
        states = diagonal(prefix_half, pair)
        for part, rows in enumerate(parts):
            start = output if side == 0 else intra
            value = start[rows, cols] + dot(q[rows, cols], states)
            output[rows, cols] = value
            terms = o[rows, cols].astype(F32) * gains[:, cols] * value
            value = value * value
            square_sums[part] = square_sums[part] + (value[:, :DH] + value[:, DH:])
            product_sums[part] = product_sums[part] + (terms[:, :DH] + terms[:, DH:])
    for part, rows in enumerate(parts):
        if side == 0:
            squares[rows, :] = square_sums[part]
            products[rows, :] = product_sums[part]
        else:
            stats[0:1, rows] = jnp.sum(square_sums[part].T, axis=0, keepdims=True)
            stats[1:2, rows] = jnp.sum(product_sums[part].T, axis=0, keepdims=True)
    if side == 0:
        wait(copies[3 * PAIRS_SIDE :])


def output_own(core, queries, out_grad, intra, intra1, gain, base, near):
    return call(
        "output0",
        functools.partial(output_body, 0),
        [SMEM] + [HBM] * 4 + [VMEM] * 3,
        [VMEM] * 9,
        [SIDE_BF16, SIDE_BF16, SIDE_F32, STATE_HALF, LANES, LANES, SIDE_BF16, SIDE_BF16, SIDE_F32],
        2 * BLOCK * SIDE * DH,
        8 * MIB,
        [pltpu.SemaphoreType.DMA((3 * PAIRS_SIDE + 3,))],
    )(core, queries, out_grad, intra, intra1, gain, base, near)


def output_other(core, q, o, intra, gain, base, near, squares, products):
    return call(
        "output1",
        functools.partial(output_body, 1),
        [SMEM] + [VMEM] * 8,
        [VMEM] * 3,
        [SIDE_F32, STATE_HALF, STATS],
        2 * BLOCK * SIDE * DH,
        MIB,
    )(core, q, o, intra, gain, base, near, squares, products)


def grad_body(side, core, q, output, o, gain, s0, s1, s2, s3, far, states, grad_out, sems):
    total = (s0[...] + s1[...]) + (s2[...] + s3[...])
    mean_square = total[0:1, :] / WIDTH_ALL + epsilon
    radius = jnp.sqrt(mean_square)
    scale = total[1:2, :] / (WIDTH_ALL * radius * radius)
    inverse = jnp.broadcast_to(1.0 / radius, (DH, BLOCK)).T
    coeff = jnp.broadcast_to(scale, (DH, BLOCK)).T
    gains = gain[:, pl.ds(side_start(core, side), SIDE)]
    copies = []
    for pair in PAIRS:
        for head in (2 * pair, 2 * pair + 1):
            cols = head_columns(head)
            scaled = o[:, cols].astype(F32) * gains[:, cols]
            grad_out[:, cols] = ((scaled - output[:, cols] * coeff) * inverse).astype(BF16)
        cols = pair_columns(pair)
        copies += copies_of([(grad_out.at[:, cols], far.at[:, cols])], sems.at[pl.ds(pair, 1)])
        store_states(states, pair, q[:, cols], grad_out[:, cols])
    wait(copies)


def local_grad(side, core, q, output, o, gain, stats):
    return call(
        f"grad{side}",
        functools.partial(grad_body, side),
        [SMEM] + [VMEM] * 8,
        [HBM, VMEM],
        [FAR_BF16, STATE],
        2 * BLOCK * SIDE * DH,
        MIB,
        [BUFFER_BF16, pltpu.SemaphoreType.DMA((PAIRS_SIDE,))],
    )(core, q, output, o, gain, *stats)


def middle_body(side, core, q_all, k_all, v_all, g_far, first_far, last_far, prefix, *refs):
    query_grad, key_far, value_far = refs[-14:-11]
    q, k, v, g, first, last, result, key_part, value_part, sems, out_sems = refs[-11:]
    before, behind = seen_keys(), seen_queries()
    copies = copies_of(
        [
            copy
            for pair in PAIRS
            for copy in (
                (v_all.at[:, pair_window(core, side, pair)], v.at[:, pair_columns(pair)]),
                (g_far.at[:, pair_columns(pair)], g.at[:, pair_columns(pair)]),
                (k_all.at[:, pair_window(core, side, pair)], k.at[:, pair_columns(pair)]),
                (q_all.at[:, pair_window(core, side, pair)], q.at[:, pair_columns(pair)]),
                (first_far.at[first_rows(pair)], first.at[first_rows(pair)]),
                (last_far.at[last_rows(pair)], last.at[last_rows(pair)]),
            )
        ],
        sems,
    )
    results = []
    for pair in PAIRS:
        wait(copies[6 * pair : 6 * pair + 6])
        across = dot_nt(g[:, pair_columns(pair)], diagonal(prefix, pair))
        for h in range(2):
            head = 2 * pair + h
            cols = head_columns(head)
            part = across[:, h * DH : (h + 1) * DH]
            mixing0, mixing1 = by_keys(before, g[:, cols], v[:, cols])
            turned0, turned1 = by_queries(behind, v[:, cols], g[:, cols])
            total = dot(last[pl.ds(head * BLOCK, BLOCK), :], g[BOTTOM, cols])
            first_total = total[TOP] + dot(first[pl.ds(head * HALF, HALF), :], g[TOP, cols])
            value_part[TOP, cols] = first_total.astype(BF16)
            value_part[BOTTOM, cols] = total[BOTTOM].astype(BF16)
            total = part + dot(mixing0, k[TOP, cols])
            result[TOP, cols] = total[TOP].astype(BF16)
            result[BOTTOM, cols] = (total[BOTTOM] + dot(mixing1, k[BOTTOM, cols])).astype(BF16)
            total = dot(turned1, q[BOTTOM, cols])
            key_part[TOP, cols] = (total[TOP] + dot(turned0, q[TOP, cols])).astype(BF16)
            key_part[BOTTOM, cols] = total[BOTTOM].astype(BF16)
        cols = pair_columns(pair)
        results += copies_of(
            [
                (result.at[:, cols], query_grad.at[:, pair_window(core, side, pair)]),
                (key_part.at[:, cols], key_far.at[:, cols]),
                (value_part.at[:, cols], value_far.at[:, cols]),
            ],
            out_sems.at[pl.ds(3 * pair, 3)],
        )
    wait(results)


def middle_gradients(side, core, queries, keys, values, g, turned, prefix, result=()):
    return call(
        f"middle{side}",
        functools.partial(middle_body, side),
        [SMEM] + [HBM] * 6 + [VMEM] + [HBM] * len(result),
        [HBM] * 3,
        [WHOLE, FAR_BF16, FAR_BF16],
        9 * BLOCK * BLOCK * SIDE,
        10 * MIB,
        [BUFFER_BF16] * 4
        + [FIRST_BUFFER, LAST_BUFFER]
        + [BUFFER_BF16] * 3
        + [pltpu.SemaphoreType.DMA((6 * PAIRS_SIDE,)), pltpu.SemaphoreType.DMA((3 * PAIRS_SIDE,))],
        {8 + i: i for i in range(len(result))},
    )(core, queries, keys, values, g, *turned, prefix, *result)


def last_body(side, core, *refs):
    if side == 0:
        k_all, v_all, key_far, value_far, key_far1, value_far1, base, near = refs[:8]
        key_grad, value_grad, k1, v1, key_part1, value_part1 = refs[8:14]
        k, v, key_part, value_part, key_half, value_half, sems, out_sems = refs[14:]
        other = pl.ds(side_start(core, 1), SIDE)
        copies = [
            (source.at[:, window], target.at[:, pair_columns(pair)])
            for pair in PAIRS
            for source, target, window in (
                (k_all, k, pair_window(core, 0, pair)),
                (v_all, v, pair_window(core, 0, pair)),
                (key_far, key_part, pair_columns(pair)),
                (value_far, value_part, pair_columns(pair)),
            )
        ]
        copies += [
            (k_all.at[:, other], k1),
            (v_all.at[:, other], v1),
            (key_far1, key_part1),
            (value_far1, value_part1),
        ]
        copies = copies_of(copies, sems)
    else:
        k, v, key_part, value_part, base, near = refs[:6]
        key_grad, value_grad, key_half, value_half, out_sems = refs[8:]
    weight = 1.0 - core[0].astype(F32)
    later = (base[...] + weight * near[...]).astype(BF16)
    results = []
    for pair in PAIRS:
        cols = pair_columns(pair)
        if side == 0:
            wait(copies[4 * pair : 4 * pair + 4])
        states = diagonal(later, pair)
        key_total = key_part[:, cols].astype(F32) + dot_nt(v[:, cols], states)
        value_total = value_part[:, cols].astype(F32) + dot(k[:, cols], states)
        key_half[:, cols] = key_total.astype(BF16)
        value_half[:, cols] = value_total.astype(BF16)
        window = pair_window(core, side, pair)
        results += copies_of(
            [(key_half.at[:, cols], key_grad.at[:, window]), (value_half.at[:, cols], value_grad.at[:, window])],
            out_sems.at[pl.ds(2 * pair, 2)],
        )
    wait(results)
    if side == 0:
        wait(copies[4 * PAIRS_SIDE :])


def last_own(core, keys, values, part, part1, base, near):
    return call(
        "last0",
        functools.partial(last_body, 0),
        [SMEM] + [HBM] * 6 + [VMEM] * 2,
        [HBM, HBM] + [VMEM] * 4,
        [WHOLE, WHOLE, SIDE_BF16, SIDE_BF16, SIDE_BF16, SIDE_BF16],
        4 * BLOCK * SIDE * DH,
        10 * MIB,
        [BUFFER_BF16] * 6
        + [pltpu.SemaphoreType.DMA((4 * PAIRS_SIDE + 4,)), pltpu.SemaphoreType.DMA((2 * PAIRS_SIDE,))],
    )(core, keys, values, *part, *part1, base, near)


def last_other(core, k, v, key_part, value_part, base, near, key_grad, value_grad):
    return call(
        "last1",
        functools.partial(last_body, 1),
        [SMEM] + [VMEM] * 6 + [HBM] * 2,
        [HBM, HBM],
        [WHOLE, WHOLE],
        4 * BLOCK * SIDE * DH,
        2 * MIB,
        [BUFFER_BF16, BUFFER_BF16, pltpu.SemaphoreType.DMA((2 * PAIRS_SIDE,))],
        {7: 0, 8: 1},
    )(core, k, v, key_part, value_part, base, near, key_grad, value_grad)


def scan_body(reverse, parts, far, out, sems):
    state = jnp.zeros((SLICE, DH), F32)
    order = range(CHIPS - 1, -1, -1) if reverse else range(CHIPS)
    for place in order:
        out[place] = state
        state = state + parts[place]
    wait(copies_of([(out, far)], sems))


def chip_scan(parts, reverse):
    return call(
        f"scan{int(reverse)}",
        functools.partial(scan_body, reverse),
        [VMEM],
        HBM,
        hbm((CHIPS, SLICE, DH), F32),
        MIB,
        MIB,
        [pltpu.VMEM((CHIPS, SLICE, DH), F32), pltpu.SemaphoreType.DMA((1,))],
    )(parts)


PARTNERS = [(i, i ^ 1) for i in range(2 * CHIPS)]
SAME_CORE = [[core + 2 * chip for chip in range(CHIPS)] for core in range(2)]


def exchange(parts):
    return lax.all_to_all(parts, "ctx", 0, 0, axis_index_groups=SAME_CORE, tiled=True)


def swap(part):
    return lax.ppermute(part, "ctx", PARTNERS)


def along_heads(stats):
    hops = (1, 2, 3)
    return [lax.ppermute(stats, "head", [(i, (i + hop) % 4) for i in range(4)]) for hop in hops]


def after(value, *done):
    return lax.optimization_barrier((value,) + done)[0]


def local(query_rows, key_rows, value_rows, out_grad, norm_gain):
    core = (lax.axis_index("ctx") % 2).astype(jnp.int32).reshape(1)
    return device(core, query_rows, key_rows, value_rows, out_grad, norm_gain)


def device(core, query_rows, key_rows, value_rows, out_grad, norm_gain):
    gain = norm_gain.reshape(1, WIDTH)
    everything = (query_rows, key_rows, value_rows)

    state1 = local_state(1, core, key_rows, value_rows)
    near0 = swap(state1)
    state0 = local_state(0, core, key_rows, value_rows)
    parts = exchange((state0 + near0).reshape(CHIPS, SLICE, DH))
    near1 = swap(state0)
    intra0, *turned0 = intra_output(0, core, *everything)
    sums = chip_scan(after(parts, intra0), False)
    base0 = exchange(sums).reshape(ROWS, DH)
    intra1, *turned1 = intra_output(1, core, *everything)
    base0 = after(base0, intra1)
    base1 = swap(base0)
    q0, o0, output0, prefix0, squares, products, q1, o1, intra1 = output_own(
        core, query_rows, out_grad, intra0, intra1, gain, base0, near0
    )
    output1, prefix1, stats = output_other(
        core, q1, o1, intra1, gain, base1, near1, squares, products
    )
    stats = [stats] + along_heads(stats)

    g1, state1 = local_grad(1, core, q1, output1, o1, gain, stats)
    near0 = swap(state1)
    g0, state0 = local_grad(0, core, q0, output0, o0, gain, stats)
    parts = exchange((state0 + near0).reshape(CHIPS, SLICE, DH))
    near1 = swap(state0)
    query_grad, *part0 = middle_gradients(0, core, *everything, g0, turned0, prefix0)
    sums = chip_scan(after(parts, *part0), True)
    base0 = exchange(sums).reshape(ROWS, DH)
    query_grad, *part1 = middle_gradients(
        1, core, *everything, g1, turned1, prefix1, (query_grad,)
    )
    base0 = after(base0, *part1)
    base1 = swap(base0)
    key_grad, value_grad, *rest = last_own(core, key_rows, value_rows, part0, part1, base0, near0)
    key_grad, value_grad = last_other(core, *rest, base1, near1, key_grad, value_grad)
    return query_grad, key_grad, value_grad


def solution(mesh):
    in_specs = (P("ctx", "head"), P("ctx", "head"), P("ctx", "head"), P("ctx", "head"), P("head"))
    out_specs = (P("ctx", "head"), P("ctx", "head"), P("ctx", "head"))
    return jax.shard_map(local, mesh=mesh, in_specs=in_specs, out_specs=out_specs, check_vma=False)
```

```python
import functools

import jax
import jax.numpy as jnp
from jax import lax
from jax.experimental import pallas as pl
from jax.experimental.pallas import tpu as pltpu
from jax.sharding import PartitionSpec as P

DH = 128
BLOCK = 512
HALF = 256
WIDTH = 2048
SIDE = WIDTH // 2
WIDTH_ALL = 8192
HEADS_SIDE = SIDE // DH
PAIRS_SIDE = HEADS_SIDE // 2
ROWS = HEADS_SIDE * DH
LINE = 4
QUARTER = ROWS // LINE
MIB = 1024 * 1024

epsilon = 1e-06

F32 = jnp.float32
BF16 = jnp.bfloat16

VMEM = pl.BlockSpec(memory_space=pltpu.VMEM)
SMEM = pl.BlockSpec(memory_space=pltpu.SMEM)
HBM = pl.BlockSpec(memory_space=pltpu.HBM)


def hbm(dims, kind):
    return pltpu.HBM(dims, kind)


SIDE_F32 = jax.ShapeDtypeStruct((BLOCK, SIDE), F32)
SIDE_BF16 = jax.ShapeDtypeStruct((BLOCK, SIDE), BF16)
STATE = jax.ShapeDtypeStruct((ROWS, DH), F32)
STATE_HALF = jax.ShapeDtypeStruct((ROWS, DH), BF16)
LANES = jax.ShapeDtypeStruct((BLOCK, DH), F32)
STATS = jax.ShapeDtypeStruct((2, BLOCK), F32)
WHOLE = hbm((BLOCK, WIDTH), BF16)
PIECE = jax.ShapeDtypeStruct((QUARTER, DH), F32)
PAIR_F32 = jax.ShapeDtypeStruct((BLOCK, 2 * DH), F32)
FIRST_SCORES = jax.ShapeDtypeStruct((HEADS_SIDE * HALF, HALF), BF16)
LAST_SCORES = jax.ShapeDtypeStruct((HEADS_SIDE * BLOCK, HALF), BF16)
BUFFER_BF16 = pltpu.VMEM((BLOCK, SIDE), BF16)


def copies_of(pairs, sems):
    copies = []
    for place, (source, target) in enumerate(pairs):
        copy = pltpu.make_async_copy(source, target, sems.at[place])
        copy.start()
        copies.append(copy)
    return copies


def wait(copies):
    for copy in copies:
        copy.wait()


def call(name, body, in_specs, out_specs, out_shape, flops, moved, scratch=(), aliases=None):
    kernel = pl.pallas_call(
        body,
        in_specs=in_specs,
        out_specs=out_specs,
        out_shape=out_shape,
        scratch_shapes=list(scratch),
        input_output_aliases=aliases or {},
        compiler_params=pltpu.CompilerParams(vmem_limit_bytes=12 * MIB),
        cost_estimate=pl.CostEstimate(flops=flops, bytes_accessed=moved, transcendentals=0),
        name=name,
    )

    def run(*arrays):
        return kernel(
            *(
                pltpu.with_memory_space_constraint(array, pltpu.HBM) if spec is HBM else array
                for spec, array in zip(in_specs, arrays)
            )
        )

    return run


def dot(a, b):
    return lax.dot_general(a, b, (((1,), (0,)), ((), ())), preferred_element_type=F32)


def dot_nt(a, b):
    return lax.dot_general(a, b, (((1,), (1,)), ((), ())), preferred_element_type=F32)


def dot_tn(a, b):
    return lax.dot_general(a, b, (((0,), (0,)), ((), ())), preferred_element_type=F32)


def pair_columns(pair):
    return slice(pair * 2 * DH, (pair + 1) * 2 * DH)


def head_columns(head):
    return slice(head * DH, (head + 1) * DH)


def diagonal(states, pair):
    first = states[2 * pair * DH : (2 * pair + 1) * DH, :]
    second = states[(2 * pair + 1) * DH : (2 * pair + 2) * DH, :]
    zero = jnp.zeros_like(first)
    return jnp.concatenate(
        [jnp.concatenate([first, zero], axis=1), jnp.concatenate([zero, second], axis=1)], axis=0
    )


def store_states(out, pair, a, b):
    both = dot_tn(a, b)
    out[2 * pair * DH : (2 * pair + 1) * DH, :] = both[:DH, :DH]
    out[(2 * pair + 1) * DH : (2 * pair + 2) * DH, :] = both[DH:, DH:]


def seen_keys():
    rows = lax.broadcasted_iota(jnp.int32, (HALF, HALF), 0)
    cols = lax.broadcasted_iota(jnp.int32, (HALF, HALF), 1)
    return cols <= rows


def seen_queries():
    rows = lax.broadcasted_iota(jnp.int32, (HALF, HALF), 0)
    cols = lax.broadcasted_iota(jnp.int32, (HALF, HALF), 1)
    return cols >= rows


def keep(mask, array):
    return jnp.where(mask, array, 0.0).astype(BF16)


TOP = slice(0, HALF)
BOTTOM = slice(HALF, BLOCK)


def by_keys(mask, queries, keys):
    first = dot_nt(queries, keys[TOP])
    last = dot_nt(queries[BOTTOM], keys[BOTTOM])
    first = jnp.concatenate([keep(mask, first[TOP]), first[BOTTOM].astype(BF16)], axis=0)
    return first, keep(mask, last)


def by_queries(mask, keys, queries):
    first = dot_nt(keys[TOP], queries[TOP])
    last = dot_nt(keys, queries[BOTTOM])
    last = jnp.concatenate([last[TOP].astype(BF16), keep(mask, last[BOTTOM])], axis=0)
    return keep(mask, first), last


def side_start(core, side):
    half = core[0] if side == 0 else 1 - core[0]
    return pl.multiple_of(half * SIDE, SIDE)


def pair_window(core, side, pair):
    return pl.ds(pl.multiple_of(side_start(core, side) + pair * 2 * DH, 2 * DH), 2 * DH)


def head_window(core, side, head):
    return pl.ds(pl.multiple_of(side_start(core, side) + head * DH, DH), DH)


PAIRS = range(PAIRS_SIDE)


def local_state_body(side, core, k_all, v_all, k, v, out, sems):
    window = pl.ds(side_start(core, side), SIDE)
    copies = copies_of(
        [
            (source.at[rows, window], target.at[rows])
            for rows in (pl.ds(0, HALF), pl.ds(HALF, HALF))
            for source, target in ((k_all, k), (v_all, v))
        ],
        sems,
    )
    for part, rows in enumerate((TOP, BOTTOM)):
        wait(copies[2 * part : 2 * part + 2])
        for pair in PAIRS:
            both = dot_tn(k[rows, pair_columns(pair)], v[rows, pair_columns(pair)])
            for h in range(2):
                place = head_columns(2 * pair + h)
                state = both[head_columns(h), head_columns(h)]
                out[place, :] = state if part == 0 else out[place, :] + state


def local_state(side, core, keys, values):
    return call(
        f"state{side}",
        functools.partial(local_state_body, side),
        [SMEM, HBM, HBM],
        [VMEM] * 3,
        [SIDE_BF16, SIDE_BF16, STATE],
        2 * BLOCK * SIDE * DH,
        2 * MIB,
        [pltpu.SemaphoreType.DMA((4,))],
    )(core, keys, values)


def intra_body(side, pairs, core, q_all, o_all, k, v, *refs):
    q, o, out, first, last, sems = refs[-6:]
    before, behind = seen_keys(), seen_queries()
    copies = copies_of(
        [
            (source.at[:, pair_window(core, side, pair)], target.at[:, pair_columns(pair)])
            for source, target in ((q_all, q), (o_all, o))
            for pair in pairs
        ],
        sems,
    )
    for place, pair in enumerate(pairs):
        wait(copies[place : place + 1])
        for head in (2 * pair, 2 * pair + 1):
            cols = head_columns(head)
            queries, keys, values = q[:, cols], k[:, cols], v[:, cols]
            scores0, scores1 = by_keys(before, queries, keys)
            first[pl.ds(head * HALF, HALF), :], last[pl.ds(head * BLOCK, BLOCK), :] = by_queries(
                behind, keys, queries
            )
            total = dot(scores0, values[TOP])
            out[TOP, cols] = total[TOP]
            out[BOTTOM, cols] = total[BOTTOM] + dot(scores1, values[BOTTOM])
    wait(copies[len(pairs) :])


def intra_output(number, side, pairs, core, queries, out_grad, k, v, begun=()):
    return call(
        f"intra{number}",
        functools.partial(intra_body, side, pairs),
        [SMEM, HBM, HBM, VMEM, VMEM] + [VMEM] * len(begun),
        [VMEM] * 5,
        [SIDE_BF16, SIDE_BF16, SIDE_F32, FIRST_SCORES, LAST_SCORES],
        5 * BLOCK * BLOCK * SIDE * len(pairs) // 4,
        2 * MIB * len(pairs),
        [pltpu.SemaphoreType.DMA((2 * len(pairs),))],
        {5 + i: i for i in range(len(begun))},
    )(core, queries, out_grad, k, v, *begun)


def output_body(side, core, q, o, intra, gain, base, near, *refs):
    if side == 0:
        output, prefix_half, squares, products = refs
    else:
        squares_in, products_in, output, prefix_half, stats = refs
    weight = core[0].astype(F32)
    gains = gain[:, pl.ds(side_start(core, side), SIDE)]
    prefix_half[...] = (base[...] + weight * near[...]).astype(BF16)
    parts = (TOP, BOTTOM)
    if side == 0:
        square_sums = [jnp.zeros((HALF, DH), F32) for rows in parts]
        product_sums = [jnp.zeros((HALF, DH), F32) for rows in parts]
    else:
        square_sums = [squares_in[rows, :] for rows in parts]
        product_sums = [products_in[rows, :] for rows in parts]
    for pair in PAIRS:
        cols = pair_columns(pair)
        states = diagonal(prefix_half, pair)
        for part, rows in enumerate(parts):
            value = intra[rows, cols] + dot(q[rows, cols], states)
            output[rows, cols] = value
            terms = o[rows, cols].astype(F32) * gains[:, cols] * value
            value = value * value
            square_sums[part] = square_sums[part] + (value[:, :DH] + value[:, DH:])
            product_sums[part] = product_sums[part] + (terms[:, :DH] + terms[:, DH:])
    for part, rows in enumerate(parts):
        if side == 0:
            squares[rows, :] = square_sums[part]
            products[rows, :] = product_sums[part]
        else:
            stats[0:1, rows] = jnp.sum(square_sums[part].T, axis=0, keepdims=True)
            stats[1:2, rows] = jnp.sum(product_sums[part].T, axis=0, keepdims=True)


def whole_output(side, core, q, o, intra, gain, base, near, sums=()):
    return call(
        f"output{side}",
        functools.partial(output_body, side),
        [SMEM] + [VMEM] * (6 + len(sums)),
        [VMEM] * (4 if side == 0 else 3),
        [SIDE_F32, STATE_HALF] + ([LANES, LANES] if side == 0 else [STATS]),
        2 * BLOCK * SIDE * DH,
        MIB,
    )(core, q, o, intra, gain, base, near, *sums)


def grad_body(side, core, q, output, o, gain, s0, s1, s2, s3, grad_out, states):
    total = (s0[...] + s1[...]) + (s2[...] + s3[...])
    mean_square = total[0:1, :] / WIDTH_ALL + epsilon
    radius = jnp.sqrt(mean_square)
    scale = total[1:2, :] / (WIDTH_ALL * radius * radius)
    inverse = jnp.broadcast_to(1.0 / radius, (DH, BLOCK)).T
    coeff = jnp.broadcast_to(scale, (DH, BLOCK)).T
    gains = gain[:, pl.ds(side_start(core, side), SIDE)]
    for pair in PAIRS:
        for head in (2 * pair, 2 * pair + 1):
            cols = head_columns(head)
            scaled = o[:, cols].astype(F32) * gains[:, cols]
            grad_out[:, cols] = ((scaled - output[:, cols] * coeff) * inverse).astype(BF16)
        cols = pair_columns(pair)
        store_states(states, pair, q[:, cols], grad_out[:, cols])


def local_grad(side, core, q, output, o, gain, stats):
    return call(
        f"grad{side}",
        functools.partial(grad_body, side),
        [SMEM] + [VMEM] * 8,
        [VMEM] * 2,
        [SIDE_BF16, STATE],
        2 * BLOCK * SIDE * DH,
        MIB,
    )(core, q, output, o, gain, *stats)


SIDE_ARRAYS = 7


def middle_body(jobs, core, *refs):
    before, behind = seen_keys(), seen_queries()
    sides = sorted({side for side, _ in jobs})
    arrays = {
        side: refs[place * SIDE_ARRAYS : (place + 1) * SIDE_ARRAYS] for place, side in enumerate(sides)
    }
    outputs = refs[len(refs) - 3 - 2 * len(jobs) :]
    query_grad, parts, result, sems = outputs[0], outputs[1:-2], outputs[-2], outputs[-1]
    results = []
    for place, (side, pair) in enumerate(jobs):
        q, k, v, g, prefix, first, last = arrays[side]
        key_part, value_part = parts[2 * place : 2 * place + 2]
        across = dot_nt(g[:, pair_columns(pair)], diagonal(prefix, pair))
        for h in range(2):
            head = 2 * pair + h
            cols, here = head_columns(head), head_columns(h)
            part = across[:, here]
            mixing0, mixing1 = by_keys(before, g[:, cols], v[:, cols])
            turned0, turned1 = by_queries(behind, v[:, cols], g[:, cols])
            total = dot(last[pl.ds(head * BLOCK, BLOCK), :], g[BOTTOM, cols])
            value_part[TOP, here] = total[TOP] + dot(first[pl.ds(head * HALF, HALF), :], g[TOP, cols])
            value_part[BOTTOM, here] = total[BOTTOM]
            there = head_columns(2 * place + h)
            total = part + dot(mixing0, k[TOP, cols])
            result[TOP, there] = total[TOP].astype(BF16)
            result[BOTTOM, there] = (total[BOTTOM] + dot(mixing1, k[BOTTOM, cols])).astype(BF16)
            total = dot(turned1, q[BOTTOM, cols])
            key_part[TOP, here] = total[TOP] + dot(turned0, q[TOP, cols])
            key_part[BOTTOM, here] = total[BOTTOM]
        results += copies_of(
            [(result.at[:, pair_columns(place)], query_grad.at[:, pair_window(core, side, pair)])],
            sems.at[pl.ds(place, 1)],
        )
    wait(results)


def middle_gradients(number, jobs, core, arrays, result=()):
    sides = sorted({side for side, _ in jobs})
    inputs = [array for side in sides for array in arrays[side]]
    query_grad, *parts = call(
        f"middle{number}",
        functools.partial(middle_body, jobs),
        [SMEM] + [VMEM] * len(inputs) + [HBM] * len(result),
        [HBM] + [VMEM] * (2 * len(jobs)),
        [WHOLE] + [PAIR_F32] * (2 * len(jobs)),
        2 * BLOCK * BLOCK * SIDE * len(jobs),
        MIB * len(jobs),
        [
            pltpu.VMEM((BLOCK, len(jobs) * 2 * DH), BF16),
            pltpu.SemaphoreType.DMA((len(jobs),)),
        ],
        {1 + len(inputs) + i: i for i in range(len(result))},
    )(core, *inputs, *result)
    return query_grad, {job: parts[2 * i : 2 * i + 2] for i, job in enumerate(jobs)}


def last_body(side, core, k, v, base, near, *refs):
    parts = refs[: 2 * PAIRS_SIDE]
    if side == 0:
        key_half, value_half = refs[2 * PAIRS_SIDE :]
    else:
        key_own, value_own, key_grad, value_grad, key_half, value_half, sems = refs[2 * PAIRS_SIDE :]
        own = pl.ds(side_start(core, 0), SIDE)
        results = copies_of(
            [(key_own, key_grad.at[:, own]), (value_own, value_grad.at[:, own])],
            sems.at[pl.ds(2 * PAIRS_SIDE, 2)],
        )
    weight = 1.0 - core[0].astype(F32)
    later = (base[...] + weight * near[...]).astype(BF16)
    for pair in PAIRS:
        cols = pair_columns(pair)
        states = diagonal(later, pair)
        key_half[:, cols] = (parts[2 * pair][...] + dot_nt(v[:, cols], states)).astype(BF16)
        value_half[:, cols] = (parts[2 * pair + 1][...] + dot(k[:, cols], states)).astype(BF16)
        if side == 1:
            window = pair_window(core, side, pair)
            results += copies_of(
                [(key_half.at[:, cols], key_grad.at[:, window]), (value_half.at[:, cols], value_grad.at[:, window])],
                sems.at[pl.ds(2 * pair, 2)],
            )
    if side == 1:
        wait(results)


def last_gradients(side, core, k, v, base, near, parts, own=()):
    inputs = [k, v, base, near] + [array for pair in PAIRS for array in parts[side, pair]] + list(own)
    return call(
        f"last{side}",
        functools.partial(last_body, side),
        [SMEM] + [VMEM] * len(inputs),
        [VMEM, VMEM] if side == 0 else [HBM, HBM],
        [SIDE_BF16, SIDE_BF16] if side == 0 else [WHOLE, WHOLE],
        4 * BLOCK * SIDE * DH,
        2 * MIB,
        []
        if side == 0
        else [BUFFER_BF16, BUFFER_BF16, pltpu.SemaphoreType.DMA((2 * PAIRS_SIDE + 2,))],
    )(core, *inputs)


def quarter(place):
    return pl.ds(pl.multiple_of(place * QUARTER, QUARTER), QUARTER)


def split_body(x, own, near, *outs):
    for hop, out in enumerate(outs):
        rows = quarter(lax.rem(x[0] + hop, LINE))
        out[...] = own[rows, :] + near[rows, :]


def split(chip, own, near):
    return call(
        "split", split_body, [SMEM, VMEM, VMEM], [VMEM] * LINE, [PIECE] * LINE, MIB, MIB
    )(chip[0], own, near)


def line_body(a, b, c, d, out):
    out[...] = (a[...] + b[...]) + (c[...] + d[...])


def line_sum(pieces):
    return call("line", line_body, [VMEM] * LINE, VMEM, PIECE, MIB, MIB)(*pieces)


def enter_body(reverse, x, y, *refs):
    pieces, sums, outs = refs[:LINE], refs[LINE : 2 * LINE - 1], refs[2 * LINE - 1 :]
    lines_ahead = LINE - 1 - y[0] if reverse else y[0]
    start = jnp.zeros((QUARTER, DH), F32)
    for hop, part in enumerate(sums, 1):
        start = start + (hop <= lines_ahead).astype(jnp.int32).astype(F32) * part[...]
    values = [piece[...] for piece in pieces]
    places = [lax.rem(x[0] + LINE - hop, LINE) for hop in range(LINE)]
    for hop, out in enumerate(outs):
        target = lax.rem(x[0] + hop, LINE)
        total = start
        for place, value in zip(places, values):
            ahead = place > target if reverse else place < target
            total = total + ahead.astype(jnp.int32).astype(F32) * value
        out[...] = total


def entering(chip, pieces, sums, reverse):
    return call(
        f"enter{int(reverse)}",
        functools.partial(enter_body, reverse),
        [SMEM] * 2 + [VMEM] * (2 * LINE - 1),
        [VMEM] * LINE,
        [PIECE] * LINE,
        MIB,
        MIB,
    )(*chip, *pieces, *sums)


def join_body(x, a, b, c, d, out):
    for hop, piece in enumerate((a, b, c, d)):
        out[quarter(lax.rem(x[0] + LINE - hop, LINE)), :] = piece[...]


def join(chip, pieces):
    return call("join", join_body, [SMEM] + [VMEM] * LINE, VMEM, STATE, MIB, MIB)(chip[0], *pieces)


def device_index(y, x, core):
    return (y * LINE + x) * 2 + core


DEVICES = [(y, x, core) for y in range(LINE) for x in range(LINE) for core in range(2)]
PARTNERS = [(i, i ^ 1) for i in range(len(DEVICES))]
HOPS = (2, 1, 3)


def along_x(pieces):
    got = {0: pieces[0]}
    for hop in HOPS:
        pairs = [
            (device_index(y, x, core), device_index(y, (x + hop) % LINE, core)) for y, x, core in DEVICES
        ]
        got[hop] = lax.ppermute(pieces[hop], "ctx", pairs)
    return [got[hop] for hop in range(LINE)]


def along_y(part, reverse):
    got = {}
    for hop in HOPS:
        step = -hop if reverse else hop
        pairs = [
            (device_index(y, x, core), device_index((y + step) % LINE, x, core)) for y, x, core in DEVICES
        ]
        got[hop] = lax.ppermute(part, "ctx", pairs)
    return [got[hop] for hop in (1, 2, 3)]


def swap(part):
    return lax.ppermute(part, "ctx", PARTNERS)


def along_heads(stats):
    hops = (1, 2, 3)
    return [lax.ppermute(stats, "head", [(i, (i + hop) % 4) for i in range(4)]) for hop in hops]


def after(value, *done):
    return lax.optimization_barrier((value,) + done)[0]


def local(query_rows, key_rows, value_rows, out_grad, norm_gain):
    place = lax.axis_index("ctx").astype(jnp.int32)
    core = (place % 2).reshape(1)
    chip = ((place // 2 % LINE).reshape(1), (place // (2 * LINE)).reshape(1))
    return device(core, chip, query_rows, key_rows, value_rows, out_grad, norm_gain)


def device(core, chip, query_rows, key_rows, value_rows, out_grad, norm_gain):
    gain = norm_gain.reshape(1, WIDTH)

    k1, v1, state1 = local_state(1, core, key_rows, value_rows)
    near0 = swap(state1)
    k0, v0, state0 = local_state(0, core, key_rows, value_rows)
    pieces = along_x(split(chip, state0, near0))
    q0, o0, intra0, *turned0 = intra_output(0, 0, PAIRS, core, query_rows, out_grad, k0, v0)
    pieces[1] = after(pieces[1], intra0)
    sums = along_y(line_sum(pieces), False)
    begun = intra_output(1, 1, PAIRS[:2], core, query_rows, out_grad, k1, v1)
    sums[0] = after(sums[0], begun[2])
    pieces = along_x(entering(chip, pieces, sums, False))
    near1 = swap(after(state0, sums[0]))
    q1, o1, intra1, *turned1 = intra_output(2, 1, PAIRS[2:], core, query_rows, out_grad, k1, v1, begun)
    pieces[1] = after(pieces[1], intra1)
    base0 = join(chip, pieces)
    base1 = swap(base0)
    output0, prefix0, *lanes = whole_output(0, core, q0, o0, intra0, gain, base0, near0)
    output1, prefix1, stats = whole_output(1, core, q1, o1, intra1, gain, base1, near1, lanes)
    stats = [stats] + along_heads(stats)

    g1, state1 = local_grad(1, core, q1, output1, o1, gain, stats)
    near0 = swap(state1)
    g0, state0 = local_grad(0, core, q0, output0, o0, gain, stats)
    arrays = ((q0, k0, v0, g0, prefix0, *turned0), (q1, k1, v1, g1, prefix1, *turned1))
    pieces = along_x(split(chip, state0, near0))
    query_grad, parts = middle_gradients(0, ((0, 0), (0, 1), (0, 2)), core, arrays)
    pieces[1] = after(pieces[1], query_grad)
    sums = along_y(line_sum(pieces), True)
    query_grad, more = middle_gradients(1, ((0, 3), (1, 0), (1, 1)), core, arrays, (query_grad,))
    parts.update(more)
    sums[0] = after(sums[0], query_grad)
    pieces = along_x(entering(chip, pieces, sums, True))
    near1 = swap(after(state0, sums[0]))
    query_grad, more = middle_gradients(2, ((1, 2), (1, 3)), core, arrays, (query_grad,))
    parts.update(more)
    pieces[1] = after(pieces[1], query_grad)
    base0 = join(chip, pieces)
    base1 = swap(base0)
    results = last_gradients(0, core, k0, v0, base0, near0, parts)
    key_grad, value_grad = last_gradients(1, core, k1, v1, base1, near1, parts, results)
    return query_grad, key_grad, value_grad


def solution(mesh):
    in_specs = (P("ctx", "head"), P("ctx", "head"), P("ctx", "head"), P("ctx", "head"), P("head"))
    out_specs = (P("ctx", "head"), P("ctx", "head"), P("ctx", "head"))
    return jax.shard_map(local, mesh=mesh, in_specs=in_specs, out_specs=out_specs, check_vma=False)
```

```python
import functools

import jax
import jax.numpy as jnp
from jax import lax
from jax.experimental import pallas as pl
from jax.experimental.pallas import tpu as pltpu
from jax.sharding import PartitionSpec as P

DH = 128
BLOCK = 512
HALF = 256
WIDTH = 2048
SIDE = WIDTH // 2
WIDTH_ALL = 8192
HEADS_SIDE = SIDE // DH
PAIRS_SIDE = HEADS_SIDE // 2
ROWS = HEADS_SIDE * DH
LINE = 4
QUARTER = ROWS // LINE
MIB = 1024 * 1024

epsilon = 1e-06

F32 = jnp.float32
BF16 = jnp.bfloat16

VMEM = pl.BlockSpec(memory_space=pltpu.VMEM)
SMEM = pl.BlockSpec(memory_space=pltpu.SMEM)
HBM = pl.BlockSpec(memory_space=pltpu.HBM)


def hbm(dims, kind):
    return pltpu.HBM(dims, kind)


SIDE_F32 = jax.ShapeDtypeStruct((BLOCK, SIDE), F32)
SIDE_BF16 = jax.ShapeDtypeStruct((BLOCK, SIDE), BF16)
STATE = jax.ShapeDtypeStruct((ROWS, DH), F32)
STATE_HALF = jax.ShapeDtypeStruct((ROWS, DH), BF16)
LANES = jax.ShapeDtypeStruct((BLOCK, DH), F32)
STATS = jax.ShapeDtypeStruct((2, BLOCK), F32)
WHOLE = hbm((BLOCK, WIDTH), BF16)
PIECE = jax.ShapeDtypeStruct((QUARTER, DH), F32)
PAIR_F32 = jax.ShapeDtypeStruct((BLOCK, 2 * DH), F32)
FIRST_SCORES = jax.ShapeDtypeStruct((HEADS_SIDE * HALF, HALF), BF16)
LAST_SCORES = jax.ShapeDtypeStruct((HEADS_SIDE * BLOCK, HALF), BF16)
BUFFER_BF16 = pltpu.VMEM((BLOCK, SIDE), BF16)


def copies_of(pairs, sems):
    copies = []
    for place, (source, target) in enumerate(pairs):
        copy = pltpu.make_async_copy(source, target, sems.at[place])
        copy.start()
        copies.append(copy)
    return copies


def wait(copies):
    for copy in copies:
        copy.wait()


def call(name, body, in_specs, out_specs, out_shape, flops, moved, scratch=(), aliases=None):
    kernel = pl.pallas_call(
        body,
        in_specs=in_specs,
        out_specs=out_specs,
        out_shape=out_shape,
        scratch_shapes=list(scratch),
        input_output_aliases=aliases or {},
        compiler_params=pltpu.CompilerParams(vmem_limit_bytes=12 * MIB),
        cost_estimate=pl.CostEstimate(flops=flops, bytes_accessed=moved, transcendentals=0),
        name=name,
    )

    def run(*arrays):
        return kernel(
            *(
                pltpu.with_memory_space_constraint(array, pltpu.HBM) if spec is HBM else array
                for spec, array in zip(in_specs, arrays)
            )
        )

    return run


def dot(a, b):
    return lax.dot_general(a, b, (((1,), (0,)), ((), ())), preferred_element_type=F32)


def dot_nt(a, b):
    return lax.dot_general(a, b, (((1,), (1,)), ((), ())), preferred_element_type=F32)


def dot_tn(a, b):
    return lax.dot_general(a, b, (((0,), (0,)), ((), ())), preferred_element_type=F32)


def pair_columns(pair):
    return slice(pair * 2 * DH, (pair + 1) * 2 * DH)


def head_columns(head):
    return slice(head * DH, (head + 1) * DH)


def diagonal(states, pair):
    first = states[2 * pair * DH : (2 * pair + 1) * DH, :]
    second = states[(2 * pair + 1) * DH : (2 * pair + 2) * DH, :]
    zero = jnp.zeros_like(first)
    return jnp.concatenate(
        [jnp.concatenate([first, zero], axis=1), jnp.concatenate([zero, second], axis=1)], axis=0
    )


def store_states(out, pair, a, b):
    both = dot_tn(a, b)
    out[2 * pair * DH : (2 * pair + 1) * DH, :] = both[:DH, :DH]
    out[(2 * pair + 1) * DH : (2 * pair + 2) * DH, :] = both[DH:, DH:]


def seen_keys():
    rows = lax.broadcasted_iota(jnp.int32, (HALF, HALF), 0)
    cols = lax.broadcasted_iota(jnp.int32, (HALF, HALF), 1)
    return cols <= rows


def seen_queries():
    rows = lax.broadcasted_iota(jnp.int32, (HALF, HALF), 0)
    cols = lax.broadcasted_iota(jnp.int32, (HALF, HALF), 1)
    return cols >= rows


def keep(mask, array):
    return jnp.where(mask, array, 0.0).astype(BF16)


TOP = slice(0, HALF)
BOTTOM = slice(HALF, BLOCK)


def by_keys(mask, queries, keys):
    first = dot_nt(queries, keys[TOP])
    last = dot_nt(queries[BOTTOM], keys[BOTTOM])
    first = jnp.concatenate([keep(mask, first[TOP]), first[BOTTOM].astype(BF16)], axis=0)
    return first, keep(mask, last)


def by_queries(mask, keys, queries):
    first = dot_nt(keys[TOP], queries[TOP])
    last = dot_nt(keys, queries[BOTTOM])
    last = jnp.concatenate([last[TOP].astype(BF16), keep(mask, last[BOTTOM])], axis=0)
    return keep(mask, first), last


def side_start(core, side):
    half = core[0] if side == 0 else 1 - core[0]
    return pl.multiple_of(half * SIDE, SIDE)


def pair_window(core, side, pair):
    return pl.ds(pl.multiple_of(side_start(core, side) + pair * 2 * DH, 2 * DH), 2 * DH)


def head_window(core, side, head):
    return pl.ds(pl.multiple_of(side_start(core, side) + head * DH, DH), DH)


PAIRS = range(PAIRS_SIDE)


def local_state_body(side, core, k_all, v_all, k, v, out, sems):
    window = pl.ds(side_start(core, side), SIDE)
    copies = copies_of(
        [
            (source.at[rows, window], target.at[rows])
            for rows in (pl.ds(0, HALF), pl.ds(HALF, HALF))
            for source, target in ((k_all, k), (v_all, v))
        ],
        sems,
    )
    for part, rows in enumerate((TOP, BOTTOM)):
        wait(copies[2 * part : 2 * part + 2])
        for pair in PAIRS:
            both = dot_tn(k[rows, pair_columns(pair)], v[rows, pair_columns(pair)])
            for h in range(2):
                place = head_columns(2 * pair + h)
                state = both[head_columns(h), head_columns(h)]
                out[place, :] = state if part == 0 else out[place, :] + state


def local_state(side, core, keys, values):
    return call(
        f"state{side}",
        functools.partial(local_state_body, side),
        [SMEM, HBM, HBM],
        [VMEM] * 3,
        [SIDE_BF16, SIDE_BF16, STATE],
        2 * BLOCK * SIDE * DH,
        2 * MIB,
        [pltpu.SemaphoreType.DMA((4,))],
    )(core, keys, values)


def intra_body(side, pairs, core, q_all, o_all, k, v, *refs):
    q, o, out, first, last, sems = refs[-6:]
    before, behind = seen_keys(), seen_queries()
    copies = copies_of(
        [
            (source.at[:, pair_window(core, side, pair)], target.at[:, pair_columns(pair)])
            for source, target in ((q_all, q), (o_all, o))
            for pair in pairs
        ],
        sems,
    )
    for place, pair in enumerate(pairs):
        wait(copies[place : place + 1])
        for head in (2 * pair, 2 * pair + 1):
            cols = head_columns(head)
            queries, keys, values = q[:, cols], k[:, cols], v[:, cols]
            scores0, scores1 = by_keys(before, queries, keys)
            first[pl.ds(head * HALF, HALF), :], last[pl.ds(head * BLOCK, BLOCK), :] = by_queries(
                behind, keys, queries
            )
            total = dot(scores0, values[TOP])
            out[TOP, cols] = total[TOP]
            out[BOTTOM, cols] = total[BOTTOM] + dot(scores1, values[BOTTOM])
    wait(copies[len(pairs) :])


def intra_output(number, side, pairs, core, queries, out_grad, k, v, begun=()):
    return call(
        f"intra{number}",
        functools.partial(intra_body, side, pairs),
        [SMEM, HBM, HBM, VMEM, VMEM] + [VMEM] * len(begun),
        [VMEM] * 5,
        [SIDE_BF16, SIDE_BF16, SIDE_F32, FIRST_SCORES, LAST_SCORES],
        5 * BLOCK * BLOCK * SIDE * len(pairs) // 4,
        2 * MIB * len(pairs),
        [pltpu.SemaphoreType.DMA((2 * len(pairs),))],
        {5 + i: i for i in range(len(begun))},
    )(core, queries, out_grad, k, v, *begun)


def output_body(side, core, q, o, intra, gain, base, *refs):
    if side == 0:
        output, prefix_half, squares, products = refs
    else:
        squares_in, products_in, output, prefix_half, stats = refs
    gains = gain[:, pl.ds(side_start(core, side), SIDE)]
    prefix_half[...] = base[...].astype(BF16)
    parts = (TOP, BOTTOM)
    if side == 0:
        square_sums = [jnp.zeros((HALF, DH), F32) for rows in parts]
        product_sums = [jnp.zeros((HALF, DH), F32) for rows in parts]
    else:
        square_sums = [squares_in[rows, :] for rows in parts]
        product_sums = [products_in[rows, :] for rows in parts]
    for pair in PAIRS:
        cols = pair_columns(pair)
        states = diagonal(prefix_half, pair)
        for part, rows in enumerate(parts):
            value = intra[rows, cols] + dot(q[rows, cols], states)
            output[rows, cols] = value
            terms = o[rows, cols].astype(F32) * gains[:, cols] * value
            value = value * value
            square_sums[part] = square_sums[part] + (value[:, :DH] + value[:, DH:])
            product_sums[part] = product_sums[part] + (terms[:, :DH] + terms[:, DH:])
    for part, rows in enumerate(parts):
        if side == 0:
            squares[rows, :] = square_sums[part]
            products[rows, :] = product_sums[part]
        else:
            stats[0:1, rows] = jnp.sum(square_sums[part].T, axis=0, keepdims=True)
            stats[1:2, rows] = jnp.sum(product_sums[part].T, axis=0, keepdims=True)


def whole_output(side, core, q, o, intra, gain, base, sums=()):
    return call(
        f"output{side}",
        functools.partial(output_body, side),
        [SMEM] + [VMEM] * (5 + len(sums)),
        [VMEM] * (4 if side == 0 else 3),
        [SIDE_F32, STATE_HALF] + ([LANES, LANES] if side == 0 else [STATS]),
        2 * BLOCK * SIDE * DH,
        MIB,
    )(core, q, o, intra, gain, base, *sums)


def grad_body(side, core, q, output, o, gain, s0, s1, s2, s3, grad_out, states):
    total = (s0[...] + s1[...]) + (s2[...] + s3[...])
    mean_square = total[0:1, :] / WIDTH_ALL + epsilon
    radius = jnp.sqrt(mean_square)
    scale = total[1:2, :] / (WIDTH_ALL * radius * radius)
    inverse = jnp.broadcast_to(1.0 / radius, (DH, BLOCK)).T
    coeff = jnp.broadcast_to(scale, (DH, BLOCK)).T
    gains = gain[:, pl.ds(side_start(core, side), SIDE)]
    for pair in PAIRS:
        for head in (2 * pair, 2 * pair + 1):
            cols = head_columns(head)
            scaled = o[:, cols].astype(F32) * gains[:, cols]
            grad_out[:, cols] = ((scaled - output[:, cols] * coeff) * inverse).astype(BF16)
        cols = pair_columns(pair)
        store_states(states, pair, q[:, cols], grad_out[:, cols])


def local_grad(side, core, q, output, o, gain, stats):
    return call(
        f"grad{side}",
        functools.partial(grad_body, side),
        [SMEM] + [VMEM] * 8,
        [VMEM] * 2,
        [SIDE_BF16, STATE],
        2 * BLOCK * SIDE * DH,
        MIB,
    )(core, q, output, o, gain, *stats)


SIDE_ARRAYS = 7


def middle_body(jobs, core, *refs):
    before, behind = seen_keys(), seen_queries()
    sides = sorted({side for side, _ in jobs})
    arrays = {
        side: refs[place * SIDE_ARRAYS : (place + 1) * SIDE_ARRAYS] for place, side in enumerate(sides)
    }
    outputs = refs[len(refs) - 3 - 2 * len(jobs) :]
    query_grad, parts, result, sems = outputs[0], outputs[1:-2], outputs[-2], outputs[-1]
    results = []
    for place, (side, pair) in enumerate(jobs):
        q, k, v, g, prefix, first, last = arrays[side]
        key_part, value_part = parts[2 * place : 2 * place + 2]
        across = dot_nt(g[:, pair_columns(pair)], diagonal(prefix, pair))
        for h in range(2):
            head = 2 * pair + h
            cols, here = head_columns(head), head_columns(h)
            part = across[:, here]
            mixing0, mixing1 = by_keys(before, g[:, cols], v[:, cols])
            turned0, turned1 = by_queries(behind, v[:, cols], g[:, cols])
            total = dot(last[pl.ds(head * BLOCK, BLOCK), :], g[BOTTOM, cols])
            value_part[TOP, here] = total[TOP] + dot(first[pl.ds(head * HALF, HALF), :], g[TOP, cols])
            value_part[BOTTOM, here] = total[BOTTOM]
            there = head_columns(2 * place + h)
            total = part + dot(mixing0, k[TOP, cols])
            result[TOP, there] = total[TOP].astype(BF16)
            result[BOTTOM, there] = (total[BOTTOM] + dot(mixing1, k[BOTTOM, cols])).astype(BF16)
            total = dot(turned1, q[BOTTOM, cols])
            key_part[TOP, here] = total[TOP] + dot(turned0, q[TOP, cols])
            key_part[BOTTOM, here] = total[BOTTOM]
        results += copies_of(
            [(result.at[:, pair_columns(place)], query_grad.at[:, pair_window(core, side, pair)])],
            sems.at[pl.ds(place, 1)],
        )
    wait(results)


def middle_gradients(number, jobs, core, arrays, result=()):
    sides = sorted({side for side, _ in jobs})
    inputs = [array for side in sides for array in arrays[side]]
    query_grad, *parts = call(
        f"middle{number}",
        functools.partial(middle_body, jobs),
        [SMEM] + [VMEM] * len(inputs) + [HBM] * len(result),
        [HBM] + [VMEM] * (2 * len(jobs)),
        [WHOLE] + [PAIR_F32] * (2 * len(jobs)),
        2 * BLOCK * BLOCK * SIDE * len(jobs),
        MIB * len(jobs),
        [
            pltpu.VMEM((BLOCK, len(jobs) * 2 * DH), BF16),
            pltpu.SemaphoreType.DMA((len(jobs),)),
        ],
        {1 + len(inputs) + i: i for i in range(len(result))},
    )(core, *inputs, *result)
    return query_grad, {job: parts[2 * i : 2 * i + 2] for i, job in enumerate(jobs)}


def last_body(side, core, k, v, base, *refs):
    parts = refs[: 2 * PAIRS_SIDE]
    key_grad, value_grad, key_half, value_half, sems = refs[-5:]
    later = base[...].astype(BF16)
    results = []
    for pair in PAIRS:
        cols = pair_columns(pair)
        states = diagonal(later, pair)
        key_half[:, cols] = (parts[2 * pair][...] + dot_nt(v[:, cols], states)).astype(BF16)
        value_half[:, cols] = (parts[2 * pair + 1][...] + dot(k[:, cols], states)).astype(BF16)
        window = pair_window(core, side, pair)
        results += copies_of(
            [(key_half.at[:, cols], key_grad.at[:, window]), (value_half.at[:, cols], value_grad.at[:, window])],
            sems.at[pl.ds(2 * pair, 2)],
        )
    wait(results)


def last_gradients(side, core, k, v, base, parts, results=()):
    inputs = [k, v, base] + [array for pair in PAIRS for array in parts[side, pair]]
    return call(
        f"last{side}",
        functools.partial(last_body, side),
        [SMEM] + [VMEM] * len(inputs) + [HBM] * len(results),
        [HBM, HBM],
        [WHOLE, WHOLE],
        4 * BLOCK * SIDE * DH,
        2 * MIB,
        [BUFFER_BF16, BUFFER_BF16, pltpu.SemaphoreType.DMA((2 * PAIRS_SIDE,))],
        {1 + len(inputs) + i: i for i in range(len(results))},
    )(core, *inputs, *results)


def quarter(place):
    return pl.ds(pl.multiple_of(place * QUARTER, QUARTER), QUARTER)


def split_body(x, own, near, *outs):
    for hop, out in enumerate(outs):
        rows = quarter(lax.rem(x[0] + hop, LINE))
        out[...] = own[rows, :] + near[rows, :]


def split(chip, own, near):
    return call(
        "split", split_body, [SMEM, VMEM, VMEM], [VMEM] * LINE, [PIECE] * LINE, MIB, MIB
    )(chip[0], own, near)


def line_body(a, b, c, d, out):
    out[...] = (a[...] + b[...]) + (c[...] + d[...])


def line_sum(pieces):
    return call("line", line_body, [VMEM] * LINE, VMEM, PIECE, MIB, MIB)(*pieces)


def enter_body(reverse, x, y, *refs):
    pieces, sums, outs = refs[:LINE], refs[LINE : 2 * LINE - 1], refs[2 * LINE - 1 :]
    lines_ahead = LINE - 1 - y[0] if reverse else y[0]
    start = jnp.zeros((QUARTER, DH), F32)
    for hop, part in enumerate(sums, 1):
        start = start + (hop <= lines_ahead).astype(jnp.int32).astype(F32) * part[...]
    values = [piece[...] for piece in pieces]
    places = [lax.rem(x[0] + LINE - hop, LINE) for hop in range(LINE)]
    for hop, out in enumerate(outs):
        target = lax.rem(x[0] + hop, LINE)
        total = start
        for place, value in zip(places, values):
            ahead = place > target if reverse else place < target
            total = total + ahead.astype(jnp.int32).astype(F32) * value
        out[...] = total


def entering(chip, pieces, sums, reverse):
    return call(
        f"enter{int(reverse)}",
        functools.partial(enter_body, reverse),
        [SMEM] * 2 + [VMEM] * (2 * LINE - 1),
        [VMEM] * LINE,
        [PIECE] * LINE,
        MIB,
        MIB,
    )(*chip, *pieces, *sums)


def join_body(reverse, x, core, a, b, c, d, own, near, here, there):
    first = core[0].astype(F32)
    second = 1.0 - first
    if reverse:
        first, second = second, first
    for hop, piece in enumerate((a, b, c, d)):
        rows = quarter(lax.rem(x[0] + LINE - hop, LINE))
        here[rows, :] = piece[...] + first * near[rows, :]
        there[rows, :] = piece[...] + second * own[rows, :]


def join(chip, core, pieces, own, near, reverse):
    here, there = call(
        f"join{int(reverse)}",
        functools.partial(join_body, reverse),
        [SMEM] * 2 + [VMEM] * (LINE + 2),
        [VMEM] * 2,
        [STATE, STATE],
        MIB,
        MIB,
    )(chip[0], core, *pieces, own, near)
    return here, swap(there)


def device_index(y, x, core):
    return (y * LINE + x) * 2 + core


DEVICES = [(y, x, core) for y in range(LINE) for x in range(LINE) for core in range(2)]
PARTNERS = [(i, i ^ 1) for i in range(len(DEVICES))]
HOPS = (2, 1, 3)


def along_x(pieces):
    got = {0: pieces[0]}
    for hop in HOPS:
        pairs = [
            (device_index(y, x, core), device_index(y, (x + hop) % LINE, core)) for y, x, core in DEVICES
        ]
        got[hop] = lax.ppermute(pieces[hop], "ctx", pairs)
    return [got[hop] for hop in range(LINE)]


def along_y(part, reverse):
    got = {}
    for hop in HOPS:
        step = -hop if reverse else hop
        pairs = [
            (device_index(y, x, core), device_index((y + step) % LINE, x, core)) for y, x, core in DEVICES
        ]
        got[hop] = lax.ppermute(part, "ctx", pairs)
    return [got[hop] for hop in (1, 2, 3)]


def swap(part):
    return lax.ppermute(part, "ctx", PARTNERS)


def along_heads(stats):
    hops = (1, 2, 3)
    return [lax.ppermute(stats, "head", [(i, (i + hop) % 4) for i in range(4)]) for hop in hops]


def after(value, *done):
    return lax.optimization_barrier((value,) + done)[0]


def local(query_rows, key_rows, value_rows, out_grad, norm_gain):
    place = lax.axis_index("ctx").astype(jnp.int32)
    core, x, y = place % 2, place // 2 % LINE, place // (2 * LINE)
    core, x, y = lax.optimization_barrier((core.reshape(1), x.reshape(1), y.reshape(1)))
    return device(core, (x, y), query_rows, key_rows, value_rows, out_grad, norm_gain)


def device(core, chip, query_rows, key_rows, value_rows, out_grad, norm_gain):
    gain = norm_gain.reshape(1, WIDTH)

    k1, v1, state1 = local_state(1, core, key_rows, value_rows)
    near0 = swap(state1)
    k0, v0, state0 = local_state(0, core, key_rows, value_rows)
    pieces = along_x(split(chip, state0, near0))
    q0, o0, intra0, *turned0 = intra_output(0, 0, PAIRS, core, query_rows, out_grad, k0, v0)
    pieces[1] = after(pieces[1], intra0)
    sums = along_y(line_sum(pieces), False)
    begun = intra_output(1, 1, PAIRS[:2], core, query_rows, out_grad, k1, v1)
    sums[0] = after(sums[0], begun[2])
    pieces = along_x(entering(chip, pieces, sums, False))
    q1, o1, intra1, *turned1 = intra_output(2, 1, PAIRS[2:], core, query_rows, out_grad, k1, v1, begun)
    pieces[1] = after(pieces[1], intra1)
    base0, base1 = join(chip, core, pieces, state0, near0, False)
    output0, prefix0, *lanes = whole_output(0, core, q0, o0, intra0, gain, base0)
    output1, prefix1, stats = whole_output(1, core, q1, o1, intra1, gain, base1, lanes)
    stats = [stats] + along_heads(stats)

    g1, state1 = local_grad(1, core, q1, output1, o1, gain, stats)
    near0 = swap(state1)
    g0, state0 = local_grad(0, core, q0, output0, o0, gain, stats)
    arrays = ((q0, k0, v0, g0, prefix0, *turned0), (q1, k1, v1, g1, prefix1, *turned1))
    pieces = along_x(split(chip, state0, near0))
    query_grad, parts = middle_gradients(0, ((0, 0), (0, 1), (0, 2)), core, arrays)
    pieces[1] = after(pieces[1], query_grad)
    sums = along_y(line_sum(pieces), True)
    query_grad, more = middle_gradients(1, ((0, 3), (1, 0), (1, 1)), core, arrays, (query_grad,))
    parts.update(more)
    sums[0] = after(sums[0], query_grad)
    pieces = along_x(entering(chip, pieces, sums, True))
    query_grad, more = middle_gradients(2, ((1, 2), (1, 3)), core, arrays, (query_grad,))
    parts.update(more)
    pieces[1] = after(pieces[1], query_grad)
    base0, base1 = join(chip, core, pieces, state0, near0, True)
    results = last_gradients(0, core, k0, v0, base0, parts)
    key_grad, value_grad = last_gradients(1, core, k1, v1, base1, parts, results)
    return query_grad, key_grad, value_grad


def solution(mesh):
    in_specs = (P("ctx", "head"), P("ctx", "head"), P("ctx", "head"), P("ctx", "head"), P("head"))
    out_specs = (P("ctx", "head"), P("ctx", "head"), P("ctx", "head"))
    return jax.shard_map(local, mesh=mesh, in_specs=in_specs, out_specs=out_specs, check_vma=False)
```

```python
import functools

import jax
import jax.numpy as jnp
from jax import lax
from jax.experimental import pallas as pl
from jax.experimental.pallas import tpu as pltpu
from jax.sharding import PartitionSpec as P

DH = 128
BLOCK = 512
HALF = 256
WIDTH = 2048
SIDE = WIDTH // 2
WIDTH_ALL = 8192
HEADS_SIDE = SIDE // DH
PAIRS_SIDE = HEADS_SIDE // 2
ROWS = HEADS_SIDE * DH
LINE = 4
QUARTER = ROWS // LINE
MIB = 1024 * 1024

epsilon = 1e-06

F32 = jnp.float32
BF16 = jnp.bfloat16

VMEM = pl.BlockSpec(memory_space=pltpu.VMEM)
SMEM = pl.BlockSpec(memory_space=pltpu.SMEM)
HBM = pl.BlockSpec(memory_space=pltpu.HBM)


def hbm(dims, kind):
    return pltpu.HBM(dims, kind)


SIDE_F32 = jax.ShapeDtypeStruct((BLOCK, SIDE), F32)
SIDE_BF16 = jax.ShapeDtypeStruct((BLOCK, SIDE), BF16)
STATE = jax.ShapeDtypeStruct((ROWS, DH), F32)
HALF_STATE = jax.ShapeDtypeStruct((ROWS // 2, DH), F32)
TURNED = jax.ShapeDtypeStruct((SIDE, BLOCK), BF16)
STATE_HALF = jax.ShapeDtypeStruct((ROWS, DH), BF16)
LANES = jax.ShapeDtypeStruct((BLOCK, DH), F32)
STATS = jax.ShapeDtypeStruct((2, BLOCK), F32)
WHOLE = hbm((BLOCK, WIDTH), BF16)
PIECE = jax.ShapeDtypeStruct((QUARTER, DH), F32)
PAIR_F32 = jax.ShapeDtypeStruct((BLOCK, 2 * DH), F32)
FIRST_SCORES = jax.ShapeDtypeStruct((HEADS_SIDE * HALF, HALF), BF16)
LAST_SCORES = jax.ShapeDtypeStruct((HEADS_SIDE * BLOCK, HALF), BF16)
BUFFER_BF16 = pltpu.VMEM((BLOCK, SIDE), BF16)


def copies_of(pairs, sems):
    copies = []
    for place, (source, target) in enumerate(pairs):
        copy = pltpu.make_async_copy(source, target, sems.at[place])
        copy.start()
        copies.append(copy)
    return copies


def wait(copies):
    for copy in copies:
        copy.wait()


def call(name, body, in_specs, out_specs, out_shape, flops, moved, scratch=(), aliases=None):
    kernel = pl.pallas_call(
        body,
        in_specs=in_specs,
        out_specs=out_specs,
        out_shape=out_shape,
        scratch_shapes=list(scratch),
        input_output_aliases=aliases or {},
        compiler_params=pltpu.CompilerParams(vmem_limit_bytes=12 * MIB),
        cost_estimate=pl.CostEstimate(flops=flops, bytes_accessed=moved, transcendentals=0),
        name=name,
    )

    def run(*arrays):
        return kernel(
            *(
                pltpu.with_memory_space_constraint(array, pltpu.HBM) if spec is HBM else array
                for spec, array in zip(in_specs, arrays)
            )
        )

    return run


def dot(a, b):
    return lax.dot_general(a, b, (((1,), (0,)), ((), ())), preferred_element_type=F32)


def dot_nt(a, b):
    return lax.dot_general(a, b, (((1,), (1,)), ((), ())), preferred_element_type=F32)


def dot_tn(a, b):
    return lax.dot_general(a, b, (((0,), (0,)), ((), ())), preferred_element_type=F32)


def pair_columns(pair):
    return slice(pair * 2 * DH, (pair + 1) * 2 * DH)


def head_columns(head):
    return slice(head * DH, (head + 1) * DH)


def diagonal(states, pair):
    first = states[2 * pair * DH : (2 * pair + 1) * DH, :]
    second = states[(2 * pair + 1) * DH : (2 * pair + 2) * DH, :]
    zero = jnp.zeros_like(first)
    return jnp.concatenate(
        [jnp.concatenate([first, zero], axis=1), jnp.concatenate([zero, second], axis=1)], axis=0
    )


def seen_keys():
    rows = lax.broadcasted_iota(jnp.int32, (HALF, HALF), 0)
    cols = lax.broadcasted_iota(jnp.int32, (HALF, HALF), 1)
    return cols <= rows


def seen_queries():
    rows = lax.broadcasted_iota(jnp.int32, (HALF, HALF), 0)
    cols = lax.broadcasted_iota(jnp.int32, (HALF, HALF), 1)
    return cols >= rows


def keep(mask, array):
    return jnp.where(mask, array, 0.0).astype(BF16)


TOP = slice(0, HALF)
BOTTOM = slice(HALF, BLOCK)


def by_keys(mask, queries, keys):
    first = dot_nt(queries, keys[TOP])
    last = dot_nt(queries[BOTTOM], keys[BOTTOM])
    first = jnp.concatenate([keep(mask, first[TOP]), first[BOTTOM].astype(BF16)], axis=0)
    return first, keep(mask, last)


def by_queries(mask, keys, queries):
    first = dot_nt(keys[TOP], queries[TOP])
    last = dot_nt(keys, queries[BOTTOM])
    last = jnp.concatenate([last[TOP].astype(BF16), keep(mask, last[BOTTOM])], axis=0)
    return keep(mask, first), last


def side_start(core, side):
    half = core[0] if side == 0 else 1 - core[0]
    return pl.multiple_of(half * SIDE, SIDE)


def pair_window(core, side, pair):
    return pl.ds(pl.multiple_of(side_start(core, side) + pair * 2 * DH, 2 * DH), 2 * DH)


def head_window(core, side, head):
    return pl.ds(pl.multiple_of(side_start(core, side) + head * DH, DH), DH)


PAIRS = range(PAIRS_SIDE)


def local_state_body(side, core, k_all, v_all, k, v, out, sems):
    window = pl.ds(side_start(core, side), SIDE)
    copies = copies_of(
        [
            (source.at[rows, window], target.at[rows])
            for rows in (pl.ds(0, HALF), pl.ds(HALF, HALF))
            for source, target in ((k_all, k), (v_all, v))
        ],
        sems,
    )
    for part, rows in enumerate((TOP, BOTTOM)):
        wait(copies[2 * part : 2 * part + 2])
        for pair in PAIRS:
            both = dot_tn(k[rows, pair_columns(pair)], v[rows, pair_columns(pair)])
            for h in range(2):
                place = head_columns(2 * pair + h)
                state = both[head_columns(h), head_columns(h)]
                out[place, :] = state if part == 0 else out[place, :] + state


def local_state(side, core, keys, values):
    return call(
        f"state{side}",
        functools.partial(local_state_body, side),
        [SMEM, HBM, HBM],
        [VMEM] * 3,
        [SIDE_BF16, SIDE_BF16, STATE],
        2 * BLOCK * SIDE * DH,
        2 * MIB,
        [pltpu.SemaphoreType.DMA((4,))],
    )(core, keys, values)


def intra_body(side, pairs, core, q_all, o_all, gain, k, v, *refs):
    q, turned, scaled, out, first, last, o, sems = refs[-8:]
    gains = gain[:, pl.ds(side_start(core, side), SIDE)]
    before, behind = seen_keys(), seen_queries()
    copies = copies_of(
        [
            (source.at[:, pair_window(core, side, pair)], target.at[:, pair_columns(pair)])
            for source, target in ((q_all, q), (o_all, o))
            for pair in pairs
        ],
        sems,
    )
    for place, pair in enumerate(pairs):
        wait(copies[place : place + 1])
        for head in (2 * pair, 2 * pair + 1):
            cols = head_columns(head)
            queries, keys, values = q[:, cols], k[:, cols], v[:, cols]
            scores0, scores1 = by_keys(before, queries, keys)
            first[pl.ds(head * HALF, HALF), :], last[pl.ds(head * BLOCK, BLOCK), :] = by_queries(
                behind, keys, queries
            )
            total = dot(scores0, values[TOP])
            out[TOP, cols] = total[TOP]
            out[BOTTOM, cols] = total[BOTTOM] + dot(scores1, values[BOTTOM])
        turned[pair_columns(pair), :] = q[:, pair_columns(pair)].T
    wait(copies[len(pairs) :])
    for pair in pairs:
        cols = pair_columns(pair)
        scaled[:, cols] = o[:, cols].astype(F32) * gains[:, cols]


def intra_output(number, side, pairs, core, queries, out_grad, gain, k, v, begun=()):
    return call(
        f"intra{number}",
        functools.partial(intra_body, side, pairs),
        [SMEM, HBM, HBM, VMEM, VMEM, VMEM] + [VMEM] * len(begun),
        [VMEM] * 6,
        [SIDE_BF16, TURNED, SIDE_F32, SIDE_F32, FIRST_SCORES, LAST_SCORES],
        5 * BLOCK * BLOCK * SIDE * len(pairs) // 4,
        2 * MIB * len(pairs),
        [BUFFER_BF16, pltpu.SemaphoreType.DMA((2 * len(pairs),))],
        {6 + i: i for i in range(len(begun))},
    )(core, queries, out_grad, gain, k, v, *begun)


def output_body(number, q, scaled, intra, base, *refs):
    pairs = (PAIRS, PAIRS[:2], PAIRS[2:])[number]
    sums_in = refs[:2] if number > 0 else ()
    if number < 2:
        output, prefix_half, squares, products = refs[-4:]
    else:
        output, prefix_half, stats = refs[-3:]
    first = head_columns(2 * pairs[0]).start
    prefix_half[first : first + len(pairs) * 2 * DH, :] = base[...].astype(BF16)
    parts = (TOP, BOTTOM)
    if number == 0:
        square_sums = [jnp.zeros((HALF, DH), F32) for rows in parts]
        product_sums = [jnp.zeros((HALF, DH), F32) for rows in parts]
    else:
        square_sums = [sums_in[0][rows, :] for rows in parts]
        product_sums = [sums_in[1][rows, :] for rows in parts]
    for pair in pairs:
        cols = pair_columns(pair)
        states = diagonal(prefix_half, pair)
        for part, rows in enumerate(parts):
            value = intra[rows, cols] + dot(q[rows, cols], states)
            output[rows, cols] = value
            terms = scaled[rows, cols] * value
            value = value * value
            square_sums[part] = square_sums[part] + (value[:, :DH] + value[:, DH:])
            product_sums[part] = product_sums[part] + (terms[:, :DH] + terms[:, DH:])
    for part, rows in enumerate(parts):
        if number < 2:
            squares[rows, :] = square_sums[part]
            products[rows, :] = product_sums[part]
        else:
            stats[0:1, rows] = jnp.sum(square_sums[part].T, axis=0, keepdims=True)
            stats[1:2, rows] = jnp.sum(product_sums[part].T, axis=0, keepdims=True)


def whole_output(number, q, scaled, intra, base, sums=(), begun=()):
    last = [STATS] if number == 2 else [LANES, LANES]
    inputs = [q, scaled, intra, base, *sums, *begun]
    return call(
        f"output{number}",
        functools.partial(output_body, number),
        [VMEM] * len(inputs),
        [VMEM] * (2 + len(last)),
        [SIDE_F32, STATE_HALF] + last,
        2 * BLOCK * SIDE * DH,
        MIB,
        (),
        {len(inputs) - len(begun) + i: i for i in range(len(begun))},
    )(*inputs)


def grad_body(turned, output, scaled, s0, s1, s2, s3, grad_out, states):
    total = (s0[...] + s1[...]) + (s2[...] + s3[...])
    mean_square = total[0:1, :] / WIDTH_ALL + epsilon
    radius = jnp.sqrt(mean_square)
    scale = total[1:2, :] / (WIDTH_ALL * radius * radius)
    inverse = jnp.broadcast_to(1.0 / radius, (DH, BLOCK)).T
    coeff = jnp.broadcast_to(scale, (DH, BLOCK)).T
    for pair in PAIRS:
        for head in (2 * pair, 2 * pair + 1):
            cols = head_columns(head)
            grad_out[:, cols] = ((scaled[:, cols] - output[:, cols] * coeff) * inverse).astype(BF16)
        both = dot(turned[pair_columns(pair), :], grad_out[:, pair_columns(pair)])
        for h in range(2):
            states[head_columns(2 * pair + h), :] = both[head_columns(h), head_columns(h)]


def local_grad(side, turned, output, scaled, stats):
    return call(
        f"grad{side}",
        grad_body,
        [VMEM] * 7,
        [VMEM] * 2,
        [SIDE_BF16, STATE],
        2 * BLOCK * SIDE * DH,
        MIB,
    )(turned, output, scaled, *stats)


SIDE_ARRAYS = 7


def middle_body(jobs, core, *refs):
    before, behind = seen_keys(), seen_queries()
    sides = sorted({side for side, _ in jobs})
    arrays = {
        side: refs[place * SIDE_ARRAYS : (place + 1) * SIDE_ARRAYS] for place, side in enumerate(sides)
    }
    outputs = refs[len(refs) - 3 - 2 * len(jobs) :]
    query_grad, parts, result, sems = outputs[0], outputs[1:-2], outputs[-2], outputs[-1]
    results = []
    for place, (side, pair) in enumerate(jobs):
        q, k, v, g, prefix, first, last = arrays[side]
        key_part, value_part = parts[2 * place : 2 * place + 2]
        across = dot_nt(g[:, pair_columns(pair)], diagonal(prefix, pair))
        for h in range(2):
            head = 2 * pair + h
            cols, here = head_columns(head), head_columns(h)
            part = across[:, here]
            mixing0, mixing1 = by_keys(before, g[:, cols], v[:, cols])
            turned0, turned1 = by_queries(behind, v[:, cols], g[:, cols])
            total = dot(last[pl.ds(head * BLOCK, BLOCK), :], g[BOTTOM, cols])
            value_part[TOP, here] = total[TOP] + dot(first[pl.ds(head * HALF, HALF), :], g[TOP, cols])
            value_part[BOTTOM, here] = total[BOTTOM]
            there = head_columns(2 * place + h)
            total = part + dot(mixing0, k[TOP, cols])
            result[TOP, there] = total[TOP].astype(BF16)
            result[BOTTOM, there] = (total[BOTTOM] + dot(mixing1, k[BOTTOM, cols])).astype(BF16)
            total = dot(turned1, q[BOTTOM, cols])
            key_part[TOP, here] = total[TOP] + dot(turned0, q[TOP, cols])
            key_part[BOTTOM, here] = total[BOTTOM]
        results += copies_of(
            [(result.at[:, pair_columns(place)], query_grad.at[:, pair_window(core, side, pair)])],
            sems.at[pl.ds(place, 1)],
        )
    wait(results)


def middle_gradients(number, jobs, core, arrays, result=()):
    sides = sorted({side for side, _ in jobs})
    inputs = [array for side in sides for array in arrays[side]]
    query_grad, *parts = call(
        f"middle{number}",
        functools.partial(middle_body, jobs),
        [SMEM] + [VMEM] * len(inputs) + [HBM] * len(result),
        [HBM] + [VMEM] * (2 * len(jobs)),
        [WHOLE] + [PAIR_F32] * (2 * len(jobs)),
        2 * BLOCK * BLOCK * SIDE * len(jobs),
        MIB * len(jobs),
        [
            pltpu.VMEM((BLOCK, len(jobs) * 2 * DH), BF16),
            pltpu.SemaphoreType.DMA((len(jobs),)),
        ],
        {1 + len(inputs) + i: i for i in range(len(result))},
    )(core, *inputs, *result)
    return query_grad, {job: parts[2 * i : 2 * i + 2] for i, job in enumerate(jobs)}


def last_body(side, core, k, v, base, *refs):
    parts = refs[: 2 * PAIRS_SIDE]
    key_grad, value_grad, key_half, value_half, sems = refs[-5:]
    later = base[...].astype(BF16)
    results = []
    for pair in PAIRS:
        cols = pair_columns(pair)
        states = diagonal(later, pair)
        key_half[:, cols] = (parts[2 * pair][...] + dot_nt(v[:, cols], states)).astype(BF16)
        value_half[:, cols] = (parts[2 * pair + 1][...] + dot(k[:, cols], states)).astype(BF16)
        window = pair_window(core, side, pair)
        results += copies_of(
            [(key_half.at[:, cols], key_grad.at[:, window]), (value_half.at[:, cols], value_grad.at[:, window])],
            sems.at[pl.ds(2 * pair, 2)],
        )
    wait(results)


def last_gradients(side, core, k, v, base, parts, results=()):
    inputs = [k, v, base] + [array for pair in PAIRS for array in parts[side, pair]]
    return call(
        f"last{side}",
        functools.partial(last_body, side),
        [SMEM] + [VMEM] * len(inputs) + [HBM] * len(results),
        [HBM, HBM],
        [WHOLE, WHOLE],
        4 * BLOCK * SIDE * DH,
        2 * MIB,
        [BUFFER_BF16, BUFFER_BF16, pltpu.SemaphoreType.DMA((2 * PAIRS_SIDE,))],
        {1 + len(inputs) + i: i for i in range(len(results))},
    )(core, *inputs, *results)


def quarter(place):
    return pl.ds(pl.multiple_of(place * QUARTER, QUARTER), QUARTER)


def split_body(x, own, near, *outs):
    for hop, out in enumerate(outs):
        rows = quarter(lax.rem(x[0] + hop, LINE))
        out[...] = own[rows, :] + near[rows, :]


def split(chip, own, near):
    return call(
        "split", split_body, [SMEM, VMEM, VMEM], [VMEM] * LINE, [PIECE] * LINE, MIB, MIB
    )(chip[0], own, near)


def line_body(a, b, c, d, out):
    out[...] = (a[...] + b[...]) + (c[...] + d[...])


def line_sum(pieces):
    return call("line", line_body, [VMEM] * LINE, VMEM, PIECE, MIB, MIB)(*pieces)


def enter_body(reverse, x, y, *refs):
    pieces, sums, outs = refs[:LINE], refs[LINE : 2 * LINE - 1], refs[2 * LINE - 1 :]
    lines_ahead = LINE - 1 - y[0] if reverse else y[0]
    start = jnp.zeros((QUARTER, DH), F32)
    for hop, part in enumerate(sums, 1):
        start = start + (hop <= lines_ahead).astype(jnp.int32).astype(F32) * part[...]
    values = [piece[...] for piece in pieces]
    places = [lax.rem(x[0] + LINE - hop, LINE) for hop in range(LINE)]
    for hop, out in enumerate(outs):
        target = lax.rem(x[0] + hop, LINE)
        total = start
        for place, value in zip(places, values):
            ahead = place > target if reverse else place < target
            total = total + ahead.astype(jnp.int32).astype(F32) * value
        out[...] = total


def entering(chip, pieces, sums, reverse):
    return call(
        f"enter{int(reverse)}",
        functools.partial(enter_body, reverse),
        [SMEM] * 2 + [VMEM] * (2 * LINE - 1),
        [VMEM] * LINE,
        [PIECE] * LINE,
        MIB,
        MIB,
    )(*chip, *pieces, *sums)


def join_body(reverse, x, core, a, b, c, d, own, near, here, *theirs):
    whole = theirs[-1]
    first = core[0].astype(F32)
    second = 1.0 - first
    if reverse:
        first, second = second, first
    for hop, piece in enumerate((a, b, c, d)):
        rows = quarter(lax.rem(x[0] + LINE - hop, LINE))
        here[rows, :] = piece[...] + first * near[rows, :]
        whole[rows, :] = piece[...] + second * own[rows, :]
    if not reverse:
        theirs[0][...] = whole[: ROWS // 2, :]
        theirs[1][...] = whole[ROWS // 2 :, :]


def join(chip, core, pieces, own, near, reverse):
    here, *theirs = call(
        f"join{int(reverse)}",
        functools.partial(join_body, reverse),
        [SMEM] * 2 + [VMEM] * (LINE + 2),
        [VMEM] * (2 if reverse else 3),
        [STATE, STATE] if reverse else [STATE, HALF_STATE, HALF_STATE],
        MIB,
        MIB,
        [] if reverse else [pltpu.VMEM((ROWS, DH), F32)],
    )(chip[0], core, *pieces, own, near)
    return (here, *map(swap, theirs))


def device_index(y, x, core):
    return (y * LINE + x) * 2 + core


DEVICES = [(y, x, core) for y in range(LINE) for x in range(LINE) for core in range(2)]
PARTNERS = [(i, i ^ 1) for i in range(len(DEVICES))]
HOPS = (2, 1, 3)


def along_x(pieces):
    got = {0: pieces[0]}
    for hop in HOPS:
        pairs = [
            (device_index(y, x, core), device_index(y, (x + hop) % LINE, core)) for y, x, core in DEVICES
        ]
        got[hop] = lax.ppermute(pieces[hop], "ctx", pairs)
    return [got[hop] for hop in range(LINE)]


def along_y(part, reverse):
    got = {}
    for hop in HOPS:
        step = -hop if reverse else hop
        pairs = [
            (device_index(y, x, core), device_index((y + step) % LINE, x, core)) for y, x, core in DEVICES
        ]
        got[hop] = lax.ppermute(part, "ctx", pairs)
    return [got[hop] for hop in (1, 2, 3)]


def swap(part):
    return lax.ppermute(part, "ctx", PARTNERS)


def along_heads(stats):
    hops = (1, 2, 3)
    return [lax.ppermute(stats, "head", [(i, (i + hop) % 4) for i in range(4)]) for hop in hops]


def after(value, *done):
    return lax.optimization_barrier((value,) + done)[0]


def local(query_rows, key_rows, value_rows, out_grad, norm_gain):
    place = lax.axis_index("ctx").astype(jnp.int32)
    core, x, y = place % 2, place // 2 % LINE, place // (2 * LINE)
    core, x, y = lax.optimization_barrier((core.reshape(1), x.reshape(1), y.reshape(1)))
    return device(core, (x, y), query_rows, key_rows, value_rows, out_grad, norm_gain)


def device(core, chip, query_rows, key_rows, value_rows, out_grad, norm_gain):
    gain = norm_gain.reshape(1, WIDTH)

    k1, v1, state1 = local_state(1, core, key_rows, value_rows)
    near0 = swap(state1)
    k0, v0, state0 = local_state(0, core, key_rows, value_rows)
    pieces = along_x(split(chip, state0, near0))
    q0, t0, scaled0, intra0, *turned0 = intra_output(
        0, 0, PAIRS, core, query_rows, out_grad, gain, k0, v0
    )
    pieces[1] = after(pieces[1], intra0)
    sums = along_y(line_sum(pieces), False)
    begun = intra_output(1, 1, PAIRS[:2], core, query_rows, out_grad, gain, k1, v1)
    sums[0] = after(sums[0], begun[3])
    pieces = along_x(entering(chip, pieces, sums, False))
    q1, t1, scaled1, intra1, *turned1 = intra_output(
        2, 1, PAIRS[2:], core, query_rows, out_grad, gain, k1, v1, begun
    )
    pieces[1] = after(pieces[1], intra1)
    base0, base1, base2 = join(chip, core, pieces, state0, near0, False)
    output0, prefix0, *lanes = whole_output(0, q0, scaled0, intra0, base0)
    *begun, squares, products = whole_output(1, q1, scaled1, intra1, base1, lanes)
    output1, prefix1, stats = whole_output(
        2, q1, scaled1, intra1, base2, (squares, products), begun
    )
    stats = [stats] + along_heads(stats)

    g1, state1 = local_grad(1, t1, output1, scaled1, stats)
    near0 = swap(state1)
    g0, state0 = local_grad(0, t0, output0, scaled0, stats)
    arrays = ((q0, k0, v0, g0, prefix0, *turned0), (q1, k1, v1, g1, prefix1, *turned1))
    pieces = along_x(split(chip, state0, near0))
    query_grad, parts = middle_gradients(0, ((0, 0), (0, 1), (0, 2)), core, arrays)
    pieces[1] = after(pieces[1], query_grad)
    sums = along_y(line_sum(pieces), True)
    query_grad, more = middle_gradients(1, ((0, 3), (1, 0), (1, 1)), core, arrays, (query_grad,))
    parts.update(more)
    sums[0] = after(sums[0], query_grad)
    pieces = along_x(entering(chip, pieces, sums, True))
    query_grad, more = middle_gradients(2, ((1, 2), (1, 3)), core, arrays, (query_grad,))
    parts.update(more)
    pieces[1] = after(pieces[1], query_grad)
    base0, base1 = join(chip, core, pieces, state0, near0, True)
    results = last_gradients(0, core, k0, v0, base0, parts)
    key_grad, value_grad = last_gradients(1, core, k1, v1, base1, parts, results)
    return query_grad, key_grad, value_grad


def solution(mesh):
    in_specs = (P("ctx", "head"), P("ctx", "head"), P("ctx", "head"), P("ctx", "head"), P("head"))
    out_specs = (P("ctx", "head"), P("ctx", "head"), P("ctx", "head"))
    return jax.shard_map(local, mesh=mesh, in_specs=in_specs, out_specs=out_specs, check_vma=False)
```

```python
import functools

import jax
import jax.numpy as jnp
from jax import lax
from jax.experimental import pallas as pl
from jax.experimental.pallas import tpu as pltpu
from jax.sharding import PartitionSpec as P

DH = 128
BLOCK = 512
HALF = 256
WIDTH = 2048
SIDE = WIDTH // 2
WIDTH_ALL = 8192
HEADS_SIDE = SIDE // DH
PAIRS_SIDE = HEADS_SIDE // 2
ROWS = HEADS_SIDE * DH
LINE = 4
QUARTER = ROWS // LINE
MIB = 1024 * 1024

epsilon = 1e-06

F32 = jnp.float32
BF16 = jnp.bfloat16

VMEM = pl.BlockSpec(memory_space=pltpu.VMEM)
SMEM = pl.BlockSpec(memory_space=pltpu.SMEM)
HBM = pl.BlockSpec(memory_space=pltpu.HBM)


def hbm(dims, kind):
    return pltpu.HBM(dims, kind)


SIDE_F32 = jax.ShapeDtypeStruct((BLOCK, SIDE), F32)
SIDE_BF16 = jax.ShapeDtypeStruct((BLOCK, SIDE), BF16)
STATE = jax.ShapeDtypeStruct((ROWS, DH), F32)
HALF_STATE = jax.ShapeDtypeStruct((ROWS // 2, DH), F32)
TURNED = jax.ShapeDtypeStruct((SIDE, BLOCK), BF16)
STATE_HALF = jax.ShapeDtypeStruct((ROWS, DH), BF16)
LANES = jax.ShapeDtypeStruct((BLOCK, DH), F32)
STATS = jax.ShapeDtypeStruct((2, BLOCK), F32)
WHOLE = hbm((BLOCK, WIDTH), BF16)
PIECE = jax.ShapeDtypeStruct((QUARTER, DH), F32)
PAIR_F32 = jax.ShapeDtypeStruct((BLOCK, 2 * DH), F32)
FIRST_SCORES = jax.ShapeDtypeStruct((HEADS_SIDE * HALF, HALF), BF16)
LAST_SCORES = jax.ShapeDtypeStruct((HEADS_SIDE * BLOCK, HALF), BF16)
BUFFER_BF16 = pltpu.VMEM((BLOCK, SIDE), BF16)


def copies_of(pairs, sems):
    copies = []
    for place, (source, target) in enumerate(pairs):
        copy = pltpu.make_async_copy(source, target, sems.at[place])
        copy.start()
        copies.append(copy)
    return copies


def wait(copies):
    for copy in copies:
        copy.wait()


def call(name, body, in_specs, out_specs, out_shape, flops, moved, scratch=(), aliases=None):
    kernel = pl.pallas_call(
        body,
        in_specs=in_specs,
        out_specs=out_specs,
        out_shape=out_shape,
        scratch_shapes=list(scratch),
        input_output_aliases=aliases or {},
        compiler_params=pltpu.CompilerParams(vmem_limit_bytes=12 * MIB),
        cost_estimate=pl.CostEstimate(flops=flops, bytes_accessed=moved, transcendentals=0),
        name=name,
    )

    def run(*arrays):
        return kernel(
            *(
                pltpu.with_memory_space_constraint(array, pltpu.HBM) if spec is HBM else array
                for spec, array in zip(in_specs, arrays)
            )
        )

    return run


def dot(a, b):
    return lax.dot_general(a, b, (((1,), (0,)), ((), ())), preferred_element_type=F32)


def dot_nt(a, b):
    return lax.dot_general(a, b, (((1,), (1,)), ((), ())), preferred_element_type=F32)


def dot_tn(a, b):
    return lax.dot_general(a, b, (((0,), (0,)), ((), ())), preferred_element_type=F32)


def pair_columns(pair):
    return slice(pair * 2 * DH, (pair + 1) * 2 * DH)


def head_columns(head):
    return slice(head * DH, (head + 1) * DH)


def diagonal(states, pair):
    first = states[2 * pair * DH : (2 * pair + 1) * DH, :]
    second = states[(2 * pair + 1) * DH : (2 * pair + 2) * DH, :]
    zero = jnp.zeros_like(first)
    return jnp.concatenate(
        [jnp.concatenate([first, zero], axis=1), jnp.concatenate([zero, second], axis=1)], axis=0
    )


def seen_keys():
    rows = lax.broadcasted_iota(jnp.int32, (HALF, HALF), 0)
    cols = lax.broadcasted_iota(jnp.int32, (HALF, HALF), 1)
    return cols <= rows


def seen_queries():
    rows = lax.broadcasted_iota(jnp.int32, (HALF, HALF), 0)
    cols = lax.broadcasted_iota(jnp.int32, (HALF, HALF), 1)
    return cols >= rows


def keep(mask, array):
    return jnp.where(mask, array, 0.0).astype(BF16)


TOP = slice(0, HALF)
BOTTOM = slice(HALF, BLOCK)


def by_keys(mask, queries, keys):
    first = dot_nt(queries, keys[TOP])
    last = dot_nt(queries[BOTTOM], keys[BOTTOM])
    first = jnp.concatenate([keep(mask, first[TOP]), first[BOTTOM].astype(BF16)], axis=0)
    return first, keep(mask, last)


def by_queries(mask, keys, queries):
    first = dot_nt(keys[TOP], queries[TOP])
    last = dot_nt(keys, queries[BOTTOM])
    last = jnp.concatenate([last[TOP].astype(BF16), keep(mask, last[BOTTOM])], axis=0)
    return keep(mask, first), last


def side_start(core, side):
    half = core[0] if side == 0 else 1 - core[0]
    return pl.multiple_of(half * SIDE, SIDE)


def pair_window(core, side, pair):
    return pl.ds(pl.multiple_of(side_start(core, side) + pair * 2 * DH, 2 * DH), 2 * DH)


def head_window(core, side, head):
    return pl.ds(pl.multiple_of(side_start(core, side) + head * DH, DH), DH)


PAIRS = range(PAIRS_SIDE)


def local_state_body(side, core, k_all, v_all, k, v, out, sems):
    window = pl.ds(side_start(core, side), SIDE)
    copies = copies_of(
        [
            (source.at[rows, window], target.at[rows])
            for rows in (pl.ds(0, HALF), pl.ds(HALF, HALF))
            for source, target in ((k_all, k), (v_all, v))
        ],
        sems,
    )
    for part, rows in enumerate((TOP, BOTTOM)):
        wait(copies[2 * part : 2 * part + 2])
        for pair in PAIRS:
            both = dot_tn(k[rows, pair_columns(pair)], v[rows, pair_columns(pair)])
            for h in range(2):
                place = head_columns(2 * pair + h)
                state = both[head_columns(h), head_columns(h)]
                out[place, :] = state if part == 0 else out[place, :] + state


def local_state(side, core, keys, values):
    return call(
        f"state{side}",
        functools.partial(local_state_body, side),
        [SMEM, HBM, HBM],
        [VMEM] * 3,
        [SIDE_BF16, SIDE_BF16, STATE],
        2 * BLOCK * SIDE * DH,
        2 * MIB,
        [pltpu.SemaphoreType.DMA((4,))],
    )(core, keys, values)


def intra_body(side, pairs, core, q_all, o_all, gain, k, v, *refs):
    q, turned, scaled, out, first, last, o, sems = refs[-8:]
    gains = gain[:, pl.ds(side_start(core, side), SIDE)]
    before, behind = seen_keys(), seen_queries()
    copies = copies_of(
        [
            (source.at[:, pair_window(core, side, pair)], target.at[:, pair_columns(pair)])
            for source, target in ((q_all, q), (o_all, o))
            for pair in pairs
        ],
        sems,
    )
    for place, pair in enumerate(pairs):
        wait(copies[place : place + 1])
        for head in (2 * pair, 2 * pair + 1):
            cols = head_columns(head)
            queries, keys, values = q[:, cols], k[:, cols], v[:, cols]
            scores0, scores1 = by_keys(before, queries, keys)
            first[pl.ds(head * HALF, HALF), :], last[pl.ds(head * BLOCK, BLOCK), :] = by_queries(
                behind, keys, queries
            )
            total = dot(scores0, values[TOP])
            out[TOP, cols] = total[TOP]
            out[BOTTOM, cols] = total[BOTTOM] + dot(scores1, values[BOTTOM])
        turned[pair_columns(pair), :] = q[:, pair_columns(pair)].T
    wait(copies[len(pairs) :])
    for pair in pairs:
        cols = pair_columns(pair)
        scaled[:, cols] = o[:, cols].astype(F32) * gains[:, cols]


def intra_output(number, side, pairs, core, queries, out_grad, gain, k, v, begun=()):
    return call(
        f"intra{number}",
        functools.partial(intra_body, side, pairs),
        [SMEM, HBM, HBM, VMEM, VMEM, VMEM] + [VMEM] * len(begun),
        [VMEM] * 6,
        [SIDE_BF16, TURNED, SIDE_F32, SIDE_F32, FIRST_SCORES, LAST_SCORES],
        5 * BLOCK * BLOCK * SIDE * len(pairs) // 4,
        2 * MIB * len(pairs),
        [BUFFER_BF16, pltpu.SemaphoreType.DMA((2 * len(pairs),))],
        {6 + i: i for i in range(len(begun))},
    )(core, queries, out_grad, gain, k, v, *begun)


def output_body(number, q, scaled, intra, base, *refs):
    pairs = (PAIRS, PAIRS[:2], PAIRS[2:])[number]
    sums_in = refs[:2] if number > 0 else ()
    if number < 2:
        output, prefix_half, squares, products = refs[-4:]
    else:
        output, prefix_half, stats = refs[-3:]
    first = head_columns(2 * pairs[0]).start
    prefix_half[first : first + len(pairs) * 2 * DH, :] = base[...].astype(BF16)
    parts = (TOP, BOTTOM)
    if number == 0:
        square_sums = [jnp.zeros((HALF, DH), F32) for rows in parts]
        product_sums = [jnp.zeros((HALF, DH), F32) for rows in parts]
    else:
        square_sums = [sums_in[0][rows, :] for rows in parts]
        product_sums = [sums_in[1][rows, :] for rows in parts]
    for pair in pairs:
        cols = pair_columns(pair)
        states = diagonal(prefix_half, pair)
        for part, rows in enumerate(parts):
            value = intra[rows, cols] + dot(q[rows, cols], states)
            output[rows, cols] = value
            terms = scaled[rows, cols] * value
            value = value * value
            square_sums[part] = square_sums[part] + (value[:, :DH] + value[:, DH:])
            product_sums[part] = product_sums[part] + (terms[:, :DH] + terms[:, DH:])
    for part, rows in enumerate(parts):
        if number < 2:
            squares[rows, :] = square_sums[part]
            products[rows, :] = product_sums[part]
        else:
            stats[0:1, rows] = jnp.sum(square_sums[part].T, axis=0, keepdims=True)
            stats[1:2, rows] = jnp.sum(product_sums[part].T, axis=0, keepdims=True)


def whole_output(number, q, scaled, intra, base, sums=(), begun=()):
    last = [STATS] if number == 2 else [LANES, LANES]
    inputs = [q, scaled, intra, base, *sums, *begun]
    return call(
        f"output{number}",
        functools.partial(output_body, number),
        [VMEM] * len(inputs),
        [VMEM] * (2 + len(last)),
        [SIDE_F32, STATE_HALF] + last,
        2 * BLOCK * SIDE * DH,
        MIB,
        (),
        {len(inputs) - len(begun) + i: i for i in range(len(begun))},
    )(*inputs)


def grad_body(turned, output, scaled, s0, s1, s2, s3, grad_out, states):
    total = (s0[...] + s1[...]) + (s2[...] + s3[...])
    mean_square = total[0:1, :] / WIDTH_ALL + epsilon
    radius = jnp.sqrt(mean_square)
    scale = total[1:2, :] / (WIDTH_ALL * radius * radius)
    inverse = jnp.broadcast_to(1.0 / radius, (DH, BLOCK)).T
    coeff = jnp.broadcast_to(scale, (DH, BLOCK)).T
    for pair in PAIRS:
        for head in (2 * pair, 2 * pair + 1):
            cols = head_columns(head)
            grad_out[:, cols] = ((scaled[:, cols] - output[:, cols] * coeff) * inverse).astype(BF16)
        both = dot(turned[pair_columns(pair), :], grad_out[:, pair_columns(pair)])
        for h in range(2):
            states[head_columns(2 * pair + h), :] = both[head_columns(h), head_columns(h)]


def local_grad(side, turned, output, scaled, stats):
    return call(
        f"grad{side}",
        grad_body,
        [VMEM] * 7,
        [VMEM] * 2,
        [SIDE_BF16, STATE],
        2 * BLOCK * SIDE * DH,
        MIB,
    )(turned, output, scaled, *stats)


SIDE_ARRAYS = 7


def middle_body(jobs, core, *refs):
    before, behind = seen_keys(), seen_queries()
    sides = sorted({side for side, _ in jobs})
    arrays = {
        side: refs[place * SIDE_ARRAYS : (place + 1) * SIDE_ARRAYS] for place, side in enumerate(sides)
    }
    outputs = refs[len(refs) - 3 - 2 * len(jobs) :]
    query_grad, parts, result, sems = outputs[0], outputs[1:-2], outputs[-2], outputs[-1]
    results = []
    for place, (side, pair) in enumerate(jobs):
        q, k, v, g, prefix, first, last = arrays[side]
        key_part, value_part = parts[2 * place : 2 * place + 2]
        across = dot_nt(g[:, pair_columns(pair)], diagonal(prefix, pair))
        for h in range(2):
            head = 2 * pair + h
            cols, here = head_columns(head), head_columns(h)
            part = across[:, here]
            mixing0, mixing1 = by_keys(before, g[:, cols], v[:, cols])
            turned0, turned1 = by_queries(behind, v[:, cols], g[:, cols])
            total = dot(last[pl.ds(head * BLOCK, BLOCK), :], g[BOTTOM, cols])
            value_part[TOP, here] = total[TOP] + dot(first[pl.ds(head * HALF, HALF), :], g[TOP, cols])
            value_part[BOTTOM, here] = total[BOTTOM]
            there = head_columns(2 * place + h)
            total = part + dot(mixing0, k[TOP, cols])
            result[TOP, there] = total[TOP].astype(BF16)
            result[BOTTOM, there] = (total[BOTTOM] + dot(mixing1, k[BOTTOM, cols])).astype(BF16)
            total = dot(turned1, q[BOTTOM, cols])
            key_part[TOP, here] = total[TOP] + dot(turned0, q[TOP, cols])
            key_part[BOTTOM, here] = total[BOTTOM]
        results += copies_of(
            [(result.at[:, pair_columns(place)], query_grad.at[:, pair_window(core, side, pair)])],
            sems.at[pl.ds(place, 1)],
        )
    wait(results)


def middle_gradients(number, jobs, core, arrays, result=()):
    sides = sorted({side for side, _ in jobs})
    inputs = [array for side in sides for array in arrays[side]]
    query_grad, *parts = call(
        f"middle{number}",
        functools.partial(middle_body, jobs),
        [SMEM] + [VMEM] * len(inputs) + [HBM] * len(result),
        [HBM] + [VMEM] * (2 * len(jobs)),
        [WHOLE] + [PAIR_F32] * (2 * len(jobs)),
        2 * BLOCK * BLOCK * SIDE * len(jobs),
        MIB * len(jobs),
        [
            pltpu.VMEM((BLOCK, len(jobs) * 2 * DH), BF16),
            pltpu.SemaphoreType.DMA((len(jobs),)),
        ],
        {1 + len(inputs) + i: i for i in range(len(result))},
    )(core, *inputs, *result)
    return query_grad, {job: parts[2 * i : 2 * i + 2] for i, job in enumerate(jobs)}


def last_body(side, core, k, v, base, *refs):
    parts = refs[: 2 * PAIRS_SIDE]
    key_grad, value_grad, key_half, value_half, sems = refs[-5:]
    later = base[...].astype(BF16)
    results = []
    for pair in PAIRS:
        cols = pair_columns(pair)
        states = diagonal(later, pair)
        key_half[:, cols] = (parts[2 * pair][...] + dot_nt(v[:, cols], states)).astype(BF16)
        value_half[:, cols] = (parts[2 * pair + 1][...] + dot(k[:, cols], states)).astype(BF16)
        window = pair_window(core, side, pair)
        results += copies_of(
            [(key_half.at[:, cols], key_grad.at[:, window]), (value_half.at[:, cols], value_grad.at[:, window])],
            sems.at[pl.ds(2 * pair, 2)],
        )
    wait(results)


def last_gradients(side, core, k, v, base, parts, results=()):
    inputs = [k, v, base] + [array for pair in PAIRS for array in parts[side, pair]]
    return call(
        f"last{side}",
        functools.partial(last_body, side),
        [SMEM] + [VMEM] * len(inputs) + [HBM] * len(results),
        [HBM, HBM],
        [WHOLE, WHOLE],
        4 * BLOCK * SIDE * DH,
        2 * MIB,
        [BUFFER_BF16, BUFFER_BF16, pltpu.SemaphoreType.DMA((2 * PAIRS_SIDE,))],
        {1 + len(inputs) + i: i for i in range(len(results))},
    )(core, *inputs, *results)


def quarter(place):
    return pl.ds(pl.multiple_of(place * QUARTER, QUARTER), QUARTER)


def split_body(x, own, near, *outs):
    for hop, out in enumerate(outs):
        rows = quarter(lax.rem(x[0] + hop, LINE))
        out[...] = own[rows, :] + near[rows, :]


def split(chip, own, near):
    return call(
        "split", split_body, [SMEM, VMEM, VMEM], [VMEM] * LINE, [PIECE] * LINE, MIB, MIB
    )(chip[0], own, near)


def line_body(a, b, c, d, out):
    out[...] = (a[...] + b[...]) + (c[...] + d[...])


def line_sum(pieces):
    return call("line", line_body, [VMEM] * LINE, VMEM, PIECE, MIB, MIB)(*pieces)


def enter_body(reverse, x, y, *refs):
    pieces, sums, outs = refs[:LINE], refs[LINE : 2 * LINE - 1], refs[2 * LINE - 1 :]
    lines_ahead = LINE - 1 - y[0] if reverse else y[0]
    start = jnp.zeros((QUARTER, DH), F32)
    for hop, part in enumerate(sums, 1):
        start = start + (hop <= lines_ahead).astype(jnp.int32).astype(F32) * part[...]
    values = [piece[...] for piece in pieces]
    places = [lax.rem(x[0] + LINE - hop, LINE) for hop in range(LINE)]
    for hop, out in enumerate(outs):
        target = lax.rem(x[0] + hop, LINE)
        total = start
        for place, value in zip(places, values):
            ahead = place > target if reverse else place < target
            total = total + ahead.astype(jnp.int32).astype(F32) * value
        out[...] = total


def entering(chip, pieces, sums, reverse):
    return call(
        f"enter{int(reverse)}",
        functools.partial(enter_body, reverse),
        [SMEM] * 2 + [VMEM] * (2 * LINE - 1),
        [VMEM] * LINE,
        [PIECE] * LINE,
        MIB,
        MIB,
    )(*chip, *pieces, *sums)


def join_body(reverse, x, core, a, b, c, d, own, near, here, *theirs):
    whole = theirs[-1]
    first = core[0].astype(F32)
    second = 1.0 - first
    if reverse:
        first, second = second, first
    for hop, piece in enumerate((a, b, c, d)):
        rows = quarter(lax.rem(x[0] + LINE - hop, LINE))
        here[rows, :] = piece[...] + first * near[rows, :]
        whole[rows, :] = piece[...] + second * own[rows, :]
    if not reverse:
        theirs[0][...] = whole[: ROWS // 2, :]
        theirs[1][...] = whole[ROWS // 2 :, :]


def join(chip, core, pieces, own, near, reverse):
    here, *theirs = call(
        f"join{int(reverse)}",
        functools.partial(join_body, reverse),
        [SMEM] * 2 + [VMEM] * (LINE + 2),
        [VMEM] * (2 if reverse else 3),
        [STATE, STATE] if reverse else [STATE, HALF_STATE, HALF_STATE],
        MIB,
        MIB,
        [] if reverse else [pltpu.VMEM((ROWS, DH), F32)],
    )(chip[0], core, *pieces, own, near)
    return (here, *map(swap, theirs))


def device_index(y, x, core):
    return (y * LINE + x) * 2 + core


DEVICES = [(y, x, core) for y in range(LINE) for x in range(LINE) for core in range(2)]
PARTNERS = [(i, i ^ 1) for i in range(len(DEVICES))]
HOPS = (2, 1, 3)


def along_x(pieces):
    got = {0: pieces[0]}
    for hop in HOPS:
        pairs = [
            (device_index(y, x, core), device_index(y, (x + hop) % LINE, core)) for y, x, core in DEVICES
        ]
        got[hop] = lax.ppermute(pieces[hop], "ctx", pairs)
    return [got[hop] for hop in range(LINE)]


def along_y(part, reverse):
    got = {}
    for hop in HOPS:
        step = -hop if reverse else hop
        pairs = [
            (device_index(y, x, core), device_index((y + step) % LINE, x, core)) for y, x, core in DEVICES
        ]
        got[hop] = lax.ppermute(part, "ctx", pairs)
    return [got[hop] for hop in (1, 2, 3)]


def swap(part):
    return lax.ppermute(part, "ctx", PARTNERS)


def along_heads(stats):
    hops = (1, 2, 3)
    return [lax.ppermute(stats, "head", [(i, (i + hop) % 4) for i in range(4)]) for hop in hops]


def after(value, *done):
    return lax.optimization_barrier((value,) + done)[0]


def local(query_rows, key_rows, value_rows, out_grad, norm_gain):
    place = lax.axis_index("ctx").astype(jnp.int32)
    core, x, y = place % 2, place // 2 % LINE, place // (2 * LINE)
    core, x, y = lax.optimization_barrier((core.reshape(1), x.reshape(1), y.reshape(1)))
    return device(core, (x, y), query_rows, key_rows, value_rows, out_grad, norm_gain)


def device(core, chip, query_rows, key_rows, value_rows, out_grad, norm_gain):
    gain = norm_gain.reshape(1, WIDTH)

    k1, v1, state1 = local_state(1, core, key_rows, value_rows)
    near0 = swap(state1)
    k0, v0, state0 = local_state(0, core, key_rows, value_rows)
    pieces = along_x(split(chip, state0, near0))
    q0, t0, scaled0, intra0, *turned0 = intra_output(
        0, 0, PAIRS, core, query_rows, out_grad, gain, k0, v0
    )
    pieces[1] = after(pieces[1], intra0)
    sums = along_y(line_sum(pieces), False)
    begun = intra_output(1, 1, PAIRS[:2], core, query_rows, out_grad, gain, k1, v1)
    sums[0] = after(sums[0], begun[3])
    pieces = along_x(entering(chip, pieces, sums, False))
    q1, t1, scaled1, intra1, *turned1 = intra_output(
        2, 1, PAIRS[2:], core, query_rows, out_grad, gain, k1, v1, begun
    )
    pieces[1] = after(pieces[1], intra1)
    base0, base1, base2 = join(chip, core, pieces, state0, near0, False)
    output0, prefix0, *lanes = whole_output(0, q0, scaled0, intra0, base0)
    *begun, squares, products = whole_output(1, q1, scaled1, intra1, base1, lanes)
    output1, prefix1, stats = whole_output(
        2, q1, scaled1, intra1, base2, (squares, products), begun
    )
    stats = [stats] + along_heads(stats)

    g1, state1 = local_grad(1, t1, output1, scaled1, stats)
    near0 = swap(state1)
    g0, state0 = local_grad(0, t0, output0, scaled0, stats)
    arrays = ((q0, k0, v0, g0, prefix0, *turned0), (q1, k1, v1, g1, prefix1, *turned1))
    pieces = along_x(split(chip, state0, near0))
    query_grad, parts = middle_gradients(0, ((0, 0), (0, 1)), core, arrays)
    pieces[1] = after(pieces[1], query_grad)
    sums = along_y(line_sum(pieces), True)
    query_grad, more = middle_gradients(1, ((0, 2), (0, 3), (1, 0)), core, arrays, (query_grad,))
    parts.update(more)
    sums[0] = after(sums[0], query_grad)
    pieces = along_x(entering(chip, pieces, sums, True))
    query_grad, more = middle_gradients(2, ((1, 1), (1, 2), (1, 3)), core, arrays, (query_grad,))
    parts.update(more)
    pieces[1] = after(pieces[1], query_grad)
    base0, base1 = join(chip, core, pieces, state0, near0, True)
    results = last_gradients(0, core, k0, v0, base0, parts)
    key_grad, value_grad = last_gradients(1, core, k1, v1, base1, parts, results)
    return query_grad, key_grad, value_grad


def solution(mesh):
    in_specs = (P("ctx", "head"), P("ctx", "head"), P("ctx", "head"), P("ctx", "head"), P("head"))
    out_specs = (P("ctx", "head"), P("ctx", "head"), P("ctx", "head"))
    return jax.shard_map(local, mesh=mesh, in_specs=in_specs, out_specs=out_specs, check_vma=False)
```
